128 devices in a mesh: lat: 4 (over z_lo, core), lon: 32 (over y, x, z_hi).
Axes of the slice: x: 4, y: 4, z: 4 (z_hi: 2, z_lo: 2; z = z_hi * 2 + z_lo), core: 2. Of those that a mesh axis runs over, the one named last changes fastest.
Arguments:
- fields_in: bfloat16 [8, 32, 1024, 512], P('lat', 'lon'), may hold values from -6 to 6
- lon_operator: bfloat16 [1024, 1024], replicated, may hold values from -0.1875 to 0.1875
- w_in: bfloat16 [512, 256], replicated, may hold values from -0.375 to 0.375
- w_out: bfloat16 [256, 512], replicated, may hold values from -0.25 to 0.25
- inverses: bfloat16 [4, 32, 32, 32, 4096], P('lat', 'lon'), may hold values from -0.5 to 1.4, as said below
- cotangent: bfloat16 [4, 32, 8, 32, 4096], P('lat', 'lon'), may hold values from -6 to 6
Outputs:
- diffused: float32 [4, 32, 8, 32, 4096], P('lat', 'lon')
- grad_fields: float32 [8, 32, 1024, 512], P('lat', 'lon')
- grad_in: float32 [512, 256], replicated
- grad_out: float32 [256, 512], replicated
The draws below stay inside these ranges and needn't reach their ends.
Inputs may be any that keep to these rules, and one draw needn't show every extreme that they name: `inverses`: the diagonal of each matrix lies between 0.6 and 1.4.
All inputs are finite; a program needn't handle non-finite values.
Results may differ from the reference program's by a relative error of at most 0.0055.
Values may be sent and summed in bfloat16 or wider, within the bound.
No kernel may reach another device: no remote copies, remote signals or barrier semaphores. Data moves between devices by JAX's collectives and lax.ppermute only.
A program may use at most 192 MiB of HBM per device.

```python
import jax
import jax.numpy as jnp
from jax import lax

FIELDS = 8
LEVELS = 32
NEURONS = 512
CLAT = 128
CLON = 32
NLAT = 512
NLON = 1024
COLS = 4096
LAT_TILES = 4
LONGITUDE_TILES = 32
VALUES = 256
N_LAT = 4
N_LON = 32


def draw_inverses(key, part):
    key = jax.random.fold_in(key, 11)
    first, second = jax.random.split(key)
    shape = (LAT_TILES, LONGITUDE_TILES, LEVELS, LEVELS, COLS)
    off_diag = jax.random.uniform(first, shape, jnp.float32, -0.5, 0.5) * (1.0 / LEVELS ** 0.5)
    diagonal = jax.random.uniform(second, shape, jnp.float32, 0.6, 1.4)
    rows = lax.broadcasted_iota(jnp.int32, shape, 2)
    cols_index = lax.broadcasted_iota(jnp.int32, shape, 3)
    return jnp.where(rows == cols_index, diagonal, off_diag).astype(jnp.bfloat16)


def block_levels(key, dims, cuts, low, largest):
    loudness = 1.0
    for position, blocks in cuts:
        heights = jax.random.uniform(jax.random.fold_in(jax.random.fold_in(key, 6), position), (blocks,), jnp.float32, low / len(cuts), largest / len(cuts))
        loudness = loudness * jnp.repeat(jnp.exp(heights), dims[position] // blocks).reshape((-1,) + (1,) * (len(dims) - 1 - position))
    return loudness


def bell_draw(rng, shape, spread, bound, cuts=(), kind=jnp.bfloat16):
    result = spread * jax.random.normal(rng, shape, jnp.float32)
    if cuts:
        result = result * block_levels(rng, shape, cuts, -0.22, 0.18)
    return jnp.clip(result, -bound, bound).astype(kind)


def setup_inputs(seed: int = 0) -> dict:
    keys = jax.random.split(jax.random.key(seed), 7)
    fields_in = bell_draw(keys[0], (FIELDS, LEVELS, NLON, NLAT), 1.0, 6.0, ((0, 4), (1, 32)))
    lon_operator = bell_draw(keys[1], (NLON, NLON), NLON ** -0.5, 0.1875)
    w_in = bell_draw(keys[2], (NEURONS, VALUES), VALUES ** -0.5, 0.375)
    w_out = bell_draw(keys[3], (VALUES, NEURONS), NEURONS ** -0.5, 0.25)
    inverses = draw_inverses(jax.random.fold_in(keys[6], 71), 0)
    cotangent = bell_draw(keys[5], (LAT_TILES, LONGITUDE_TILES, FIELDS, LEVELS, COLS), 1.0, 6.0, ((0, 4), (1, 32)))
    return {"fields_in": fields_in, "lon_operator": lon_operator, "w_in": w_in, "w_out": w_out, "inverses": inverses, "cotangent": cotangent}


KAPPA = 0.2


def silu_slope(value):
    sig = jax.nn.sigmoid(value)
    return sig * (1.0 + value * (1.0 - sig))


def meridional(field):
    padded_field = jnp.pad(field, ((0, 0), (0, 0), (1, 1)))
    return padded_field[:, :, 2:] + padded_field[:, :, :-2] - 2.0 * field


def dynamics(fields_in, lon_operator):
    wide_operator = lon_operator.astype(jnp.float32)

    def one_field(block):
        wide_block = block.astype(jnp.float32)
        along_longitude = jnp.einsum("gay,az->gzy", wide_block, wide_operator)
        return wide_block + along_longitude + KAPPA * meridional(wide_block)
    return lax.map(one_field, fields_in)


def adjoint_dynamics(grad_adv, lon_operator):
    wide_operator = lon_operator.astype(jnp.float32)

    def one_field(block):
        wide_block = block.astype(jnp.float32)
        along_longitude = jnp.einsum("ueh,fe->ufh", wide_block, wide_operator)
        return wide_block + along_longitude + KAPPA * meridional(wide_block)
    return lax.map(one_field, grad_adv)


def split_into_tiles(grid):
    shaped = grid.reshape(FIELDS, LEVELS, N_LON, CLON, N_LAT, CLAT)
    return shaped.transpose(4, 2, 0, 1, 3, 5).reshape(N_LAT * N_LON, FIELDS, LEVELS, COLS)


def to_grid(tiles):
    shaped = tiles.reshape(N_LAT, N_LON, FIELDS, LEVELS, CLON, CLAT)
    return shaped.transpose(2, 3, 1, 4, 0, 5).reshape(FIELDS, LEVELS, NLON, NLAT)


def reference(fields_in, lon_operator, w_in, w_out, inverses, cotangent):
    advanced = dynamics(fields_in, lon_operator).astype(jnp.bfloat16)
    columns = split_into_tiles(advanced)
    inv_tiles = inverses.reshape(N_LAT * N_LON, LEVELS, LEVELS, COLS)
    cot_tiles = cotangent.reshape(N_LAT * N_LON, FIELDS, LEVELS, COLS)

    def tile_step(carry, items):
        column, matrix, incoming = items
        flat = column.reshape(VALUES, COLS)
        pre_act = jnp.dot(w_in, flat, preferred_element_type=jnp.float32)
        activity = jax.nn.silu(pre_act).astype(jnp.bfloat16)
        mixed = (flat.astype(jnp.float32) + jnp.dot(w_out, activity, preferred_element_type=jnp.float32)).astype(jnp.bfloat16)
        mixed = mixed.reshape(FIELDS, LEVELS, COLS)
        wide_matrix = matrix.astype(jnp.float32)
        diffused = jnp.einsum("lmc,fmc->flc", wide_matrix, mixed.astype(jnp.float32))
        grad_mixed = jnp.einsum("lmc,flc->fmc", wide_matrix, incoming.astype(jnp.float32)).reshape(VALUES, COLS)
        grad_mixed_b = grad_mixed.astype(jnp.bfloat16)
        grad_act = jnp.dot(w_out.T, grad_mixed_b, preferred_element_type=jnp.float32)
        grad_pre = (grad_act * silu_slope(pre_act)).astype(jnp.bfloat16)
        grad_columns = (grad_mixed + jnp.dot(w_in.T, grad_pre, preferred_element_type=jnp.float32)).astype(jnp.bfloat16)
        grad_in = carry[0] + jnp.dot(grad_pre, flat.T, preferred_element_type=jnp.float32)
        grad_out = carry[1] + jnp.dot(grad_mixed_b, activity.T, preferred_element_type=jnp.float32)
        return (grad_in, grad_out), (diffused, grad_columns.reshape(FIELDS, LEVELS, COLS))

    start = (jnp.zeros((NEURONS, VALUES), jnp.float32), jnp.zeros((VALUES, NEURONS), jnp.float32))
    (grad_in, grad_out), (diffused, grad_columns) = lax.scan(tile_step, start, (columns, inv_tiles, cot_tiles))
    grad_fields = adjoint_dynamics(to_grid(grad_columns), lon_operator)
    diffused = diffused.reshape(N_LAT, N_LON, FIELDS, LEVELS, COLS)
    return diffused, grad_fields, grad_in, grad_out
```

```python
import functools

import jax
import jax.numpy as jnp
from jax import lax
from jax.experimental import pallas as pl
from jax.experimental.pallas import tpu as pltpu
from jax.sharding import PartitionSpec as P

KAPPA = 0.2
AXES = ("lat", "lon")
BF = jnp.bfloat16
F32 = jnp.float32
LANES = 128
QROWS = 8
VMEM_LIMIT = 60 * 1024 * 1024


def params():
    return pltpu.CompilerParams(vmem_limit_bytes=VMEM_LIMIT)


def cost(flops, nbytes, trans=0):
    return pl.CostEstimate(flops=int(flops), bytes_accessed=int(nbytes), transcendentals=int(trans))


def dot(a, b, dims=(1, 0)):
    return lax.dot_general(a, b, (((dims[0],), (dims[1],)), ((), ())), preferred_element_type=F32)


def meridional(wide):
    size = wide.shape[1]
    lane = lax.broadcasted_iota(jnp.int32, wide.shape, 1)
    before = jnp.where(lane == 0, 0.0, pltpu.roll(wide, 1, 1))
    after = jnp.where(lane == size - 1, 0.0, pltpu.roll(wide, size - 1, 1))
    return after + before - 2.0 * wide


def forward_kernel(v_ref, op_ref, out_ref, *, block):
    step = pl.program_id(0)
    rows = pl.ds(pl.multiple_of(step * block, block), block)
    fields = v_ref.shape[0]
    tiles, tile_lon, chunks = out_ref.shape[0], out_ref.shape[1], out_ref.shape[2]
    done = []
    for f in range(fields):
        along = dot(op_ref[...], v_ref[f], (0, 0))
        wide = v_ref[f, rows, :].astype(F32)
        done.append(wide + along + KAPPA * meridional(wide))
    for a in range(tiles):
        parts = [
            d[:, a * LANES : (a + 1) * LANES].reshape(tile_lon, chunks, 1, QROWS, LANES) for d in done
        ]
        joined = jnp.concatenate(parts, axis=2).reshape(tile_lon, chunks, fields * QROWS, LANES)
        out_ref[a] = joined.astype(BF)


def forward(fields_in, operator, lat_tiles, lon_tiles, tile_lon):
    fields, grid_lon, grid_lat = fields_in.shape
    chunks = tile_lon // QROWS
    block = 256
    out_shape = (lat_tiles, lon_tiles, chunks, fields * QROWS, LANES)
    return pl.pallas_call(
        functools.partial(forward_kernel, block=block),
        grid=(grid_lon // block,),
        in_specs=[
            pl.BlockSpec((fields, grid_lon, grid_lat), lambda i: (0, 0, 0)),
            pl.BlockSpec((grid_lon, block), lambda i: (0, i)),
        ],
        out_specs=pl.BlockSpec(
            (lat_tiles, block // tile_lon) + out_shape[2:], lambda i: (0, i, 0, 0, 0)
        ),
        out_shape=jax.ShapeDtypeStruct(out_shape, BF),
        compiler_params=params(),
        cost_estimate=cost(2 * fields * grid_lon * grid_lon * grid_lat, 6 << 20),
        name="forward_dynamics",
    )(fields_in, operator)


def grad_mixed_kernel(inv_ref, cot_ref, out_ref, wide):
    levels = inv_ref.shape[0]
    fields = cot_ref.shape[0] // levels
    wide[...] = cot_ref[...].astype(F32)

    def tile(t, carry):
        lanes = pl.ds(pl.multiple_of(t * LANES, LANES), LANES)
        acc = [None] * fields
        for l in range(levels):
            matrix = inv_ref[l, :, lanes].astype(F32)
            for f in range(fields):
                term = matrix * wide[pl.ds(f * levels + l, 1), lanes]
                acc[f] = term if acc[f] is None else acc[f] + term
        for f in range(fields):
            out_ref[f * levels : (f + 1) * levels, lanes] = acc[f]
        return carry

    lax.fori_loop(0, inv_ref.shape[2] // LANES, tile, 0)


def grad_mixed_of(matrix, incoming):
    levels, _, columns = matrix.shape
    values = incoming.shape[0]
    chunk = 512
    return pl.pallas_call(
        grad_mixed_kernel,
        grid=(columns // chunk,),
        in_specs=[
            pl.BlockSpec((levels, levels, chunk), lambda i: (0, 0, i)),
            pl.BlockSpec((values, chunk), lambda i: (0, i)),
        ],
        out_specs=pl.BlockSpec((values, chunk), lambda i: (0, i)),
        out_shape=jax.ShapeDtypeStruct((values, columns), F32),
        scratch_shapes=[pltpu.VMEM((values, chunk), F32)],
        compiler_params=params(),
        cost_estimate=cost(2 * values * levels * columns, 16 << 20),
        name="grad_mixed",
    )(matrix, incoming)


def network_kernel(
    arrived_ref, gm_ref, w_in_ref, w_out_t_ref, w_in_t_ref,
    leaving_ref, cols_ref, act_ref, wide, acc_in, acc_out, *, steps, tiles,
):
    step = pl.program_id(0)
    sources, rows = arrived_ref.shape[0], arrived_ref.shape[2]
    fields = rows // QROWS
    group = sources // tiles

    @pl.when(step == 0)
    def _():
        acc_in[...] = jnp.zeros_like(acc_in)
        acc_out[...] = jnp.zeros_like(acc_out)

    @pl.when(step < steps)
    def _():
        wide[...] = arrived_ref[:, 0].astype(F32).reshape(sources * rows, LANES)
        for q in range(QROWS):
            by_field = [wide[pl.ds(f * QROWS + q, sources, stride=rows), :] for f in range(fields)]
            parts = [
                by_field[f][a * group : (a + 1) * group] for a in range(tiles) for f in range(fields)
            ]
            cols_ref[:, q * LANES : (q + 1) * LANES] = jnp.concatenate(parts, axis=0).astype(BF)
        width = 256
        for j in range(QROWS * LANES // width):
            lanes = slice(j * width, (j + 1) * width)
            cols = cols_ref[:, lanes]
            pre = dot(w_in_ref[...], cols)
            sig = 0.5 + 0.5 * jnp.tanh(0.5 * pre)
            act = pre * sig
            act_b = act.astype(BF)
            act_ref[:, lanes] = act_b
            gm = gm_ref[:, lanes]
            gm_b = gm.astype(BF)
            grad_act = dot(w_out_t_ref[...], gm_b)
            grad_pre = (grad_act * (sig + act * (1.0 - sig))).astype(BF)
            grad_cols = gm + dot(w_in_t_ref[...], grad_pre)
            for k in range(width // LANES):
                q = j * (width // LANES) + k
                piece = grad_cols[:, k * LANES : (k + 1) * LANES]
                for f in range(fields):
                    parts = [
                        piece[(a * fields + f) * group : (a * fields + f + 1) * group]
                        for a in range(tiles)
                    ]
                    wide[pl.ds(f * QROWS + q, sources, stride=rows), :] = jnp.concatenate(parts, axis=0)
            acc_in[...] += dot(grad_pre, cols, (1, 1))
            acc_out[...] += dot(gm_b, act_b, (1, 1))
        leaving_ref[:, 0] = wide[...].reshape(sources, rows, LANES).astype(BF)

    @pl.when(step == steps)
    def _():
        place = 0
        for acc in (acc_in, acc_out):
            height, breadth = acc.shape
            for j in range(breadth // LANES):
                count = height // rows
                part = acc[:, j * LANES : (j + 1) * LANES].reshape(count, rows, LANES)
                leaving_ref[place : place + count, 0] = part.astype(BF)
                place += count


def network(arrived, grad_mixed, w_in, w_out_t, w_in_t, tiles):
    sources, steps, rows, _ = arrived.shape
    values, columns = grad_mixed.shape
    neurons = w_in.shape[0]
    chunk = columns // steps
    last = steps - 1
    whole = lambda i: (0, 0)
    return pl.pallas_call(
        functools.partial(network_kernel, steps=steps, tiles=tiles),
        grid=(steps + 1,),
        in_specs=[
            pl.BlockSpec((sources, 1, rows, LANES), lambda i: (0, jnp.minimum(i, last), 0, 0)),
            pl.BlockSpec((values, chunk), lambda i: (0, jnp.minimum(i, last))),
            pl.BlockSpec((neurons, values), whole),
            pl.BlockSpec((neurons, values), whole),
            pl.BlockSpec((values, neurons), whole),
        ],
        out_specs=[
            pl.BlockSpec((sources, 1, rows, LANES), lambda i: (0, i, 0, 0)),
            pl.BlockSpec((values, chunk), lambda i: (0, jnp.minimum(i, last))),
            pl.BlockSpec((neurons, chunk), lambda i: (0, jnp.minimum(i, last))),
        ],
        out_shape=[
            jax.ShapeDtypeStruct((sources, steps + 1, rows, LANES), BF),
            jax.ShapeDtypeStruct((values, columns), BF),
            jax.ShapeDtypeStruct((neurons, columns), BF),
        ],
        scratch_shapes=[
            pltpu.VMEM((sources * rows, LANES), F32),
            pltpu.VMEM((neurons, values), F32),
            pltpu.VMEM((values, neurons), F32),
        ],
        compiler_params=params(),
        cost_estimate=cost(10 * neurons * values * columns, 16 << 20, neurons * columns),
        name="column_network",
    )(arrived, grad_mixed, w_in, w_out_t, w_in_t)


def diffused_kernel(cols_ref, act_ref, w_out_ref, inv_ref, out_ref, mixed, flat):
    fields, levels = out_ref.shape[0], out_ref.shape[1]
    total = cols_ref[...].astype(F32) + dot(w_out_ref[...], act_ref[...])
    mixed[...] = total.astype(BF).astype(F32)

    def tile(t, carry):
        lanes = pl.ds(pl.multiple_of(t * LANES, LANES), LANES)
        flat[...] = inv_ref[:, :, lanes].astype(F32).reshape(levels * levels, LANES)
        acc = [None] * fields
        for m in range(levels):
            matrix = flat[pl.ds(m, levels, stride=levels), :]
            for f in range(fields):
                term = matrix * mixed[pl.ds(f * levels + m, 1), lanes]
                acc[f] = term if acc[f] is None else acc[f] + term
        for f in range(fields):
            out_ref[f, :, lanes] = acc[f]
        return carry

    lax.fori_loop(0, inv_ref.shape[2] // LANES, tile, 0)


def diffused_of(cols, act, w_out, matrix, fields):
    levels, _, columns = matrix.shape
    values, neurons = w_out.shape
    chunk = 512
    return pl.pallas_call(
        diffused_kernel,
        grid=(columns // chunk,),
        in_specs=[
            pl.BlockSpec((values, chunk), lambda i: (0, i)),
            pl.BlockSpec((neurons, chunk), lambda i: (0, i)),
            pl.BlockSpec((values, neurons), lambda i: (0, 0)),
            pl.BlockSpec((levels, levels, chunk), lambda i: (0, 0, i)),
        ],
        out_specs=pl.BlockSpec((fields, levels, chunk), lambda i: (0, 0, i)),
        out_shape=jax.ShapeDtypeStruct((fields, levels, columns), F32),
        scratch_shapes=[
            pltpu.VMEM((values, chunk), F32),
            pltpu.VMEM((levels * levels, LANES), F32),
        ],
        compiler_params=params(),
        cost_estimate=cost(2 * values * (levels + neurons) * columns, 20 << 20),
        name="diffused",
    )(cols, act, w_out, matrix)


def adjoint_kernel(back_ref, op_ref, out_ref, grid_ref, *, block):
    step = pl.program_id(0)
    fields = out_ref.shape[0]
    tiles, lon_tiles, chunks = back_ref.shape[:3]

    @pl.when(step == 0)
    def _():
        for a in range(tiles):
            wide = back_ref[a].astype(F32).reshape(lon_tiles * chunks, fields, QROWS, LANES)
            for f in range(fields):
                grid_ref[f, :, a * LANES : (a + 1) * LANES] = (
                    wide[:, f].reshape(lon_tiles * chunks * QROWS, LANES).astype(BF)
                )

    rows = pl.ds(pl.multiple_of(step * block, block), block)
    for f in range(fields):
        along = dot(op_ref[...], grid_ref[f])
        wide = grid_ref[f, rows, :].astype(F32)
        out_ref[f] = wide + along + KAPPA * meridional(wide)


def adjoint(returned, operator, fields, grid_lat):
    tiles, lon_tiles, _, rows, _ = returned.shape
    grid_lon = operator.shape[0]
    chunks = grid_lon // (lon_tiles * QROWS)
    block = 256
    return pl.pallas_call(
        functools.partial(adjoint_kernel, block=block),
        grid=(grid_lon // block,),
        in_specs=[
            pl.BlockSpec((tiles, lon_tiles, chunks, rows, LANES), lambda i: (0, 0, 0, 0, 0)),
            pl.BlockSpec((block, grid_lon), lambda i: (i, 0)),
        ],
        out_specs=pl.BlockSpec((fields, block, grid_lat), lambda i: (0, i, 0)),
        out_shape=jax.ShapeDtypeStruct((fields, grid_lon, grid_lat), F32),
        scratch_shapes=[pltpu.VMEM((fields, grid_lon, grid_lat), BF)],
        compiler_params=params(),
        cost_estimate=cost(2 * fields * grid_lon * grid_lon * grid_lat, 8 << 20),
        name="adjoint_dynamics",
    )(returned, operator)


def weight_sum_kernel(parts_ref, _, out_ref):
    total = jnp.sum(parts_ref[:, 0].astype(F32), axis=0, keepdims=True)
    out_ref[...] = jnp.broadcast_to(total.astype(BF), out_ref.shape)


def weight_sum(returned, after):
    sources, chunks, rows, _ = returned.shape
    return pl.pallas_call(
        weight_sum_kernel,
        grid=(1,),
        in_specs=[
            pl.BlockSpec((sources, 1, rows, LANES), lambda i: (0, chunks - 1, 0, 0)),
            pl.BlockSpec(memory_space=pl.ANY),
        ],
        out_specs=pl.BlockSpec((sources, rows, LANES), lambda i: (0, 0, 0)),
        out_shape=jax.ShapeDtypeStruct((sources, rows, LANES), BF),
        compiler_params=params(),
        cost_estimate=cost(sources * rows * LANES, 1 << 20),
        name="weight_sum",
    )(returned, after)


def weight_spread_kernel(shares_ref, in_ref, out_ref):
    rows = shares_ref.shape[1]
    place = 0
    for ref in (in_ref, out_ref):
        height, breadth = ref.shape
        for j in range(breadth // LANES):
            count = height // rows
            part = shares_ref[place : place + count].astype(F32)
            ref[:, j * LANES : (j + 1) * LANES] = part.reshape(height, LANES)
            place += count


def weight_spread(shares, neurons, values):
    return pl.pallas_call(
        weight_spread_kernel,
        out_shape=[
            jax.ShapeDtypeStruct((neurons, values), F32),
            jax.ShapeDtypeStruct((values, neurons), F32),
        ],
        compiler_params=params(),
        name="weight_spread",
    )(shares)


def exchange(array):
    return lax.all_to_all(array, AXES, split_axis=0, concat_axis=0, tiled=True)


def per_device(fields_in, lon_operator, w_in, w_out, inverses, cotangent):
    lat_tiles = lax.axis_size("lat")
    lon_tiles = lax.axis_size("lon")
    devices = lat_tiles * lon_tiles
    field_dev, _, grid_lon, grid_lat = fields_in.shape
    all_fields, all_levels, columns = cotangent.shape[2:]
    neurons, values = w_in.shape
    tile_lon = grid_lon // lon_tiles

    leaving = forward(
        fields_in.reshape(field_dev, grid_lon, grid_lat), lon_operator, lat_tiles, lon_tiles, tile_lon
    )
    arrived = exchange(leaving.reshape((devices,) + leaving.shape[2:]))

    matrix = inverses.reshape(all_levels, all_levels, columns)
    grad_mixed = grad_mixed_of(matrix, cotangent.reshape(values, columns))

    going, cols, act = network(arrived, grad_mixed, w_in, w_out.T, w_in.T, lat_tiles)
    returned = exchange(going)

    diffused = diffused_of(cols, act, w_out, matrix, all_fields)

    shares = exchange(weight_sum(returned, diffused))
    grad_fields = adjoint(
        returned.reshape((lat_tiles, lon_tiles) + returned.shape[1:]), lon_operator, field_dev, grid_lat
    )
    grad_in, grad_out = weight_spread(shares, neurons, values)
    return (
        diffused.reshape(1, 1, all_fields, all_levels, columns),
        grad_fields.reshape(field_dev, 1, grid_lon, grid_lat),
        grad_in,
        grad_out,
    )


def solution(mesh):
    in_specs = (
        P("lat", "lon", None, None),
        P(),
        P(),
        P(),
        P("lat", "lon", None, None, None),
        P("lat", "lon", None, None, None),
    )
    out_specs = (P("lat", "lon", None, None, None), P("lat", "lon", None, None), P(), P())
    return jax.shard_map(
        per_device, mesh=mesh, in_specs=in_specs, out_specs=out_specs, check_vma=False
    )
```

```python
import functools

import jax
import jax.numpy as jnp
from jax import lax
from jax.experimental import pallas as pl
from jax.experimental.pallas import tpu as pltpu
from jax.sharding import PartitionSpec as P

KAPPA = 0.2
AXES = ("lat", "lon")
BF = jnp.bfloat16
F32 = jnp.float32
LANES = 128
QROWS = 8
VMEM_LIMIT = 60 * 1024 * 1024


def params():
    return pltpu.CompilerParams(vmem_limit_bytes=VMEM_LIMIT)


def cost(flops, nbytes, trans=0):
    return pl.CostEstimate(flops=int(flops), bytes_accessed=int(nbytes), transcendentals=int(trans))


def dot(a, b, dims=(1, 0)):
    return lax.dot_general(a, b, (((dims[0],), (dims[1],)), ((), ())), preferred_element_type=F32)


def spread(wide):
    size = wide.shape[1]
    lane = lax.broadcasted_iota(jnp.int32, wide.shape, 1)
    before = jnp.where(lane == 0, 0.0, pltpu.roll(wide, 1, 1))
    after = jnp.where(lane == size - 1, 0.0, pltpu.roll(wide, size - 1, 1))
    return (1.0 - 2.0 * KAPPA) * wide + KAPPA * (after + before)


def forward_kernel(v_hbm, op_hbm, out_hbm, v_ref, op_ref, out_ref, v_sem, op_sem, out_sem):
    fields = v_ref.shape[0]
    blocks = op_ref.shape[0]
    block = op_ref.shape[2]
    tiles, _, chunks, rows, _ = out_ref.shape
    tile_lon = chunks * QROWS
    per_block = block // tile_lon

    def fetch_op(i):
        return pltpu.make_async_copy(op_hbm.at[:, pl.ds(i * block, block)], op_ref.at[i], op_sem.at[i])

    def fetch_v(f):
        return pltpu.make_async_copy(v_hbm.at[f], v_ref.at[f], v_sem.at[f])

    def store(i):
        part = pl.ds(i * per_block, per_block)
        return pltpu.make_async_copy(out_ref.at[:, part], out_hbm.at[:, part], out_sem.at[i])

    fetch_op(0).start()
    for f in range(fields):
        fetch_v(f).start()
    for i in range(1, blocks):
        fetch_op(i).start()
    def step(i, carry):
        fetch_op(i).wait()

        @pl.when(i == 0)
        def _():
            for f in range(fields):
                fetch_v(f).wait()

        rows_here = pl.ds(pl.multiple_of(i * block, block), block)
        done = []
        for f in range(fields):
            along = dot(op_ref[i], v_ref[f], (0, 0))
            wide = v_ref[f, rows_here, :].astype(F32)
            done.append(along + spread(wide))
        for a in range(tiles):
            parts = [
                d[:, a * LANES : (a + 1) * LANES].reshape(per_block, chunks, 1, QROWS, LANES)
                for d in done
            ]
            joined = jnp.concatenate(parts, axis=2).reshape(per_block, chunks, rows, LANES)
            out_ref[a, pl.ds(i * per_block, per_block)] = joined.astype(BF)
        store(i).start()
        return carry

    lax.fori_loop(0, blocks, step, 0)
    for i in range(blocks):
        store(i).wait()


def forward(fields_in, operator, lat_tiles, lon_tiles, tile_lon):
    fields, grid_lon, grid_lat = fields_in.shape
    chunks = tile_lon // QROWS
    block = 256
    blocks = grid_lon // block
    out_shape = (lat_tiles, lon_tiles, chunks, fields * QROWS, LANES)
    return pl.pallas_call(
        forward_kernel,
        in_specs=[pl.BlockSpec(memory_space=pltpu.HBM)] * 2,
        out_specs=pl.BlockSpec(memory_space=pltpu.HBM),
        out_shape=jax.ShapeDtypeStruct(out_shape, BF),
        scratch_shapes=[
            pltpu.VMEM(fields_in.shape, BF),
            pltpu.VMEM((blocks, grid_lon, block), BF),
            pltpu.VMEM(out_shape, BF),
            pltpu.SemaphoreType.DMA((fields,)),
            pltpu.SemaphoreType.DMA((blocks,)),
            pltpu.SemaphoreType.DMA((blocks,)),
        ],
        compiler_params=params(),
        cost_estimate=cost(2 * fields * grid_lon * grid_lon * grid_lat, 6 << 20),
        name="forward_dynamics",
    )(fields_in, operator)


def grad_mixed_kernel(inv_ref, cot_ref, out_ref, wide):
    levels = inv_ref.shape[0]
    fields = cot_ref.shape[0] // levels
    wide[...] = cot_ref[...].astype(F32)

    def tile(t, carry):
        lanes = pl.ds(pl.multiple_of(t * LANES, LANES), LANES)
        acc = [None] * fields
        for l in range(levels):
            matrix = inv_ref[l, :, lanes].astype(F32)
            for f in range(fields):
                term = matrix * wide[pl.ds(f * levels + l, 1), lanes]
                acc[f] = term if acc[f] is None else acc[f] + term
        for f in range(fields):
            out_ref[f * levels : (f + 1) * levels, lanes] = acc[f].astype(BF)
        return carry

    lax.fori_loop(0, inv_ref.shape[2] // LANES, tile, 0)


def grad_mixed_of(matrix, incoming):
    levels, _, columns = matrix.shape
    values = incoming.shape[0]
    chunk = 512
    return pl.pallas_call(
        grad_mixed_kernel,
        grid=(columns // chunk,),
        in_specs=[
            pl.BlockSpec((levels, levels, chunk), lambda i: (0, 0, i)),
            pl.BlockSpec((values, chunk), lambda i: (0, i)),
        ],
        out_specs=pl.BlockSpec((values, chunk), lambda i: (0, i)),
        out_shape=jax.ShapeDtypeStruct((values, columns), BF),
        scratch_shapes=[pltpu.VMEM((values, chunk), F32)],
        compiler_params=params(),
        cost_estimate=cost(2 * values * levels * columns, 16 << 20),
        name="grad_mixed",
    )(matrix, incoming)


def network_kernel(
    arrived_hbm, gm_hbm, w_half_hbm, w_out_hbm,
    leaving_hbm, cols_hbm,
    arrived, gm, w_half, w_out, leaving, cols, act, grad_pre, wide_in, wide_out, acc_in, acc_out,
    in_sem, w_sem, out_sem, *, tiles,
):
    sources, steps, rows, _ = arrived_hbm.shape
    fields = rows // QROWS
    group = sources // tiles
    chunk = QROWS * LANES

    def fetch(i):
        lanes = pl.ds(i * chunk, chunk)
        return (
            pltpu.make_async_copy(arrived_hbm.at[:, i], arrived.at[i], in_sem.at[0, i]),
            pltpu.make_async_copy(gm_hbm.at[:, lanes], gm.at[i], in_sem.at[1, i]),
        )

    def fetch_weights():
        return [
            pltpu.make_async_copy(w_half_hbm, w_half, w_sem.at[0]),
            pltpu.make_async_copy(w_out_hbm, w_out, w_sem.at[1]),
        ]

    def store_leaving(i):
        return pltpu.make_async_copy(leaving.at[i], leaving_hbm.at[:, i], out_sem.at[0, i])

    def store_cols(i):
        return pltpu.make_async_copy(
            cols.at[i], cols_hbm.at[:, pl.ds(i * chunk, chunk)], out_sem.at[1, i]
        )

    weights = fetch_weights()
    first = fetch(0)
    first[0].start()
    weights[0].start()
    first[1].start()
    weights[1].start()
    for i in range(1, steps):
        for copy in fetch(i):
            copy.start()
    acc_in[...] = jnp.zeros_like(acc_in)
    acc_out[...] = jnp.zeros_like(acc_out)
    for copy in weights:
        copy.wait()

    def step(i, carry):
        for copy in fetch(i):
            copy.wait()
        wide_in[...] = arrived[i].astype(F32).reshape(sources * rows, LANES)
        for q in range(QROWS):
            by_field = [
                wide_in[pl.ds(f * QROWS + q, sources, stride=rows), :] for f in range(fields)
            ]
            parts = [
                by_field[f][a * group : (a + 1) * group] for a in range(tiles) for f in range(fields)
            ]
            cols[i, :, q * LANES : (q + 1) * LANES] = jnp.concatenate(parts, axis=0).astype(BF)
        half = dot(w_half[...], cols[i])
        turn = jnp.tanh(half)
        value = half + half * turn
        act[...] = value.astype(BF)
        slope = 1.0 + (turn + value) - turn * value
        grad_pre[...] = (dot(w_out[...], gm[i], (0, 0)) * slope).astype(BF)
        grad_cols = gm[i].astype(F32) + dot(w_half[...], grad_pre[...], (0, 0))
        acc_in[...] += dot(grad_pre[...], cols[i], (1, 1))
        acc_out[...] += dot(act[...], gm[i], (1, 1))
        for q in range(QROWS):
            piece = grad_cols[:, q * LANES : (q + 1) * LANES]
            for f in range(fields):
                parts = [
                    piece[(a * fields + f) * group : (a * fields + f + 1) * group]
                    for a in range(tiles)
                ]
                wide_out[pl.ds(f * QROWS + q, sources, stride=rows), :] = jnp.concatenate(
                    parts, axis=0
                )
        leaving[i] = wide_out[...].reshape(sources, rows, LANES).astype(BF)
        store_cols(i).start()
        store_leaving(i).start()
        return carry

    lax.fori_loop(0, steps, step, 0)
    total_in = 0.5 * acc_in[...]
    total_out = acc_out[...]
    place = 0
    for total in (total_in, total_out):
        height, breadth = total.shape
        for j in range(breadth // LANES):
            count = height // rows
            part = total[:, j * LANES : (j + 1) * LANES].reshape(count, rows, LANES)
            leaving[steps, place : place + count] = part.astype(BF)
            place += count
    store_leaving(steps).start()
    for i in range(steps):
        store_cols(i).wait()
        store_leaving(i).wait()
    store_leaving(steps).wait()


def network(arrived, grad_mixed, w_half, w_out, tiles):
    sources, steps, rows, _ = arrived.shape
    values, columns = grad_mixed.shape
    neurons = w_half.shape[0]
    chunk = columns // steps
    return pl.pallas_call(
        functools.partial(network_kernel, tiles=tiles),
        in_specs=[pl.BlockSpec(memory_space=pltpu.HBM)] * 4,
        out_specs=[pl.BlockSpec(memory_space=pltpu.HBM)] * 2,
        out_shape=[
            jax.ShapeDtypeStruct((sources, steps + 1, rows, LANES), BF),
            jax.ShapeDtypeStruct((values, columns), BF),
        ],
        scratch_shapes=[
            pltpu.VMEM((steps, sources, rows, LANES), BF),
            pltpu.VMEM((steps, values, chunk), BF),
            pltpu.VMEM((neurons, values), BF),
            pltpu.VMEM((values, neurons), BF),
            pltpu.VMEM((steps + 1, sources, rows, LANES), BF),
            pltpu.VMEM((steps, values, chunk), BF),
            pltpu.VMEM((neurons, chunk), BF),
            pltpu.VMEM((neurons, chunk), BF),
            pltpu.VMEM((sources * rows, LANES), F32),
            pltpu.VMEM((sources * rows, LANES), F32),
            pltpu.VMEM((neurons, values), F32),
            pltpu.VMEM((neurons, values), F32),
            pltpu.SemaphoreType.DMA((2, steps)),
            pltpu.SemaphoreType.DMA((2,)),
            pltpu.SemaphoreType.DMA((2, steps + 1)),
        ],
        compiler_params=params(),
        cost_estimate=cost(8 * neurons * values * columns, 14 << 20, neurons * columns),
        name="column_network",
    )(arrived, grad_mixed, w_half, w_out)


def diffused_kernel(cols_ref, w_half_ref, w_out_ref, inv_ref, out_ref, mixed, flat):
    fields, levels = out_ref.shape[0], out_ref.shape[1]
    half = dot(w_half_ref[...], cols_ref[...])
    act = (half + half * jnp.tanh(half)).astype(BF)
    total = cols_ref[...].astype(F32) + dot(w_out_ref[...], act)
    mixed[...] = total.astype(BF).astype(F32)

    def tile(t, carry):
        lanes = pl.ds(pl.multiple_of(t * LANES, LANES), LANES)
        flat[...] = inv_ref[:, :, lanes].astype(F32).reshape(levels * levels, LANES)
        acc = [None] * fields
        for m in range(levels):
            matrix = flat[pl.ds(m, levels, stride=levels), :]
            for f in range(fields):
                term = matrix * mixed[pl.ds(f * levels + m, 1), lanes]
                acc[f] = term if acc[f] is None else acc[f] + term
        for f in range(fields):
            out_ref[f, :, lanes] = acc[f]
        return carry

    lax.fori_loop(0, inv_ref.shape[2] // LANES, tile, 0)


def diffused_of(cols, w_half, w_out, matrix, fields):
    levels, _, columns = matrix.shape
    values, neurons = w_out.shape
    chunk = 512
    return pl.pallas_call(
        diffused_kernel,
        grid=(columns // chunk,),
        in_specs=[
            pl.BlockSpec((values, chunk), lambda i: (0, i)),
            pl.BlockSpec((neurons, values), lambda i: (0, 0)),
            pl.BlockSpec((values, neurons), lambda i: (0, 0)),
            pl.BlockSpec((levels, levels, chunk), lambda i: (0, 0, i)),
        ],
        out_specs=pl.BlockSpec((fields, levels, chunk), lambda i: (0, 0, i)),
        out_shape=jax.ShapeDtypeStruct((fields, levels, columns), F32),
        scratch_shapes=[
            pltpu.VMEM((values, chunk), F32),
            pltpu.VMEM((levels * levels, LANES), F32),
        ],
        compiler_params=params(),
        cost_estimate=cost(2 * values * (levels + 2 * neurons) * columns, 16 << 20),
        name="diffused",
    )(cols, w_half, w_out, matrix)


def adjoint_kernel(back_hbm, op_hbm, out_hbm, back, op_ref, grid_ref, out_ref, back_sem, op_sem, out_sem):
    fields = out_ref.shape[0]
    tiles, lon_tiles, chunks, rows, _ = back.shape
    grid_lon = grid_ref.shape[1]
    block = 256
    blocks = grid_lon // block

    def fetch_back(a):
        return pltpu.make_async_copy(back_hbm.at[a, :, pl.ds(0, chunks)], back.at[a], back_sem.at[a])

    def fetch_op(i):
        part = pl.ds(i * block, block)
        return pltpu.make_async_copy(op_hbm.at[part], op_ref.at[part], op_sem.at[i])

    def store(f, i):
        part = pl.ds(i * block, block)
        return pltpu.make_async_copy(out_ref.at[f, part], out_hbm.at[f, part], out_sem.at[f, i])

    for a in range(tiles):
        fetch_back(a).start()
    for i in range(blocks):
        fetch_op(i).start()
    for a in range(tiles):
        fetch_back(a).wait()
        wide = back[a].astype(F32).reshape(lon_tiles * chunks, fields, QROWS, LANES)
        for f in range(fields):
            grid_ref[f, :, a * LANES : (a + 1) * LANES] = (
                wide[:, f].reshape(grid_lon, LANES).astype(BF)
            )
    def step(i, carry):
        fetch_op(i).wait()
        part = pl.ds(pl.multiple_of(i * block, block), block)
        for f in range(fields):
            along = dot(op_ref[part, :], grid_ref[f])
            wide = grid_ref[f, part, :].astype(F32)
            out_ref[f, part, :] = along + spread(wide)
            store(f, i).start()
        return carry

    lax.fori_loop(0, blocks, step, 0)
    for i in range(blocks):
        for f in range(fields):
            store(f, i).wait()


def adjoint(returned, operator, fields, grid_lat):
    tiles, lon_tiles, _, rows, _ = returned.shape
    grid_lon = operator.shape[0]
    chunks = grid_lon // (lon_tiles * QROWS)
    blocks = grid_lon // 256
    return pl.pallas_call(
        adjoint_kernel,
        in_specs=[pl.BlockSpec(memory_space=pltpu.HBM)] * 2,
        out_specs=pl.BlockSpec(memory_space=pltpu.HBM),
        out_shape=jax.ShapeDtypeStruct((fields, grid_lon, grid_lat), F32),
        scratch_shapes=[
            pltpu.VMEM((tiles, lon_tiles, chunks, rows, LANES), BF),
            pltpu.VMEM(operator.shape, BF),
            pltpu.VMEM((fields, grid_lon, grid_lat), BF),
            pltpu.VMEM((fields, grid_lon, grid_lat), F32),
            pltpu.SemaphoreType.DMA((tiles,)),
            pltpu.SemaphoreType.DMA((blocks,)),
            pltpu.SemaphoreType.DMA((fields, blocks)),
        ],
        compiler_params=params(),
        cost_estimate=cost(2 * fields * grid_lon * grid_lon * grid_lat, 8 << 20),
        name="adjoint_dynamics",
    )(returned, operator)


def weight_sum_kernel(returned_hbm, _, out_hbm, parts, out_ref, in_sem, out_sem):
    pieces = in_sem.shape[0]
    each = parts.shape[0] // pieces
    last = returned_hbm.shape[1] - 1

    def fetch(k):
        part = pl.ds(k * each, each)
        return pltpu.make_async_copy(returned_hbm.at[part, last], parts.at[part], in_sem.at[k])

    for k in range(pieces):
        fetch(k).start()
    total = None
    for k in range(pieces):
        fetch(k).wait()
        piece = jnp.sum(parts[k * each : (k + 1) * each].astype(F32), axis=0, keepdims=True)
        total = piece if total is None else total + piece
    out_ref[...] = jnp.broadcast_to(total.astype(BF), out_ref.shape)
    store = pltpu.make_async_copy(out_ref, out_hbm, out_sem)
    store.start()
    store.wait()


def weight_sum(returned, after):
    sources, _, rows, _ = returned.shape
    shape = (sources, rows, LANES)
    return pl.pallas_call(
        weight_sum_kernel,
        in_specs=[pl.BlockSpec(memory_space=pltpu.HBM)] * 2,
        out_specs=pl.BlockSpec(memory_space=pltpu.HBM),
        out_shape=jax.ShapeDtypeStruct(shape, BF),
        scratch_shapes=[
            pltpu.VMEM(shape, BF),
            pltpu.VMEM(shape, BF),
            pltpu.SemaphoreType.DMA((4,)),
            pltpu.SemaphoreType.DMA,
        ],
        compiler_params=params(),
        cost_estimate=cost(sources * rows * LANES, 1 << 20),
        name="weight_sum",
    )(returned, after)


def weight_spread_kernel(shares_hbm, in_hbm, out_hbm, shares, in_ref, out_ref, in_sem, out_sem):
    rows = shares.shape[1]
    height, breadth = in_ref.shape
    count = height // rows
    each = breadth // LANES
    jobs = 2 * each

    def fetch(k):
        part = pl.ds(k * count, count)
        return pltpu.make_async_copy(shares_hbm.at[part], shares.at[part], in_sem.at[k])

    def store(k):
        part = pl.ds((k % each) * LANES, LANES)
        if k < each:
            return pltpu.make_async_copy(in_ref.at[:, part], in_hbm.at[:, part], out_sem.at[k])
        return pltpu.make_async_copy(out_ref.at[part], out_hbm.at[part], out_sem.at[k])

    for k in range(jobs):
        fetch(k).start()
    for k in range(jobs):
        fetch(k).wait()
        wide = shares[k * count : (k + 1) * count].astype(F32).reshape(height, LANES)
        part = slice((k % each) * LANES, (k % each + 1) * LANES)
        if k < each:
            in_ref[:, part] = wide
        else:
            out_ref[part, :] = wide.T
        store(k).start()
    for k in range(jobs):
        store(k).wait()


def weight_spread(shares, neurons, values):
    shapes = [(neurons, values), (values, neurons)]
    jobs = 2 * (values // LANES)
    return pl.pallas_call(
        weight_spread_kernel,
        in_specs=[pl.BlockSpec(memory_space=pltpu.HBM)],
        out_specs=[pl.BlockSpec(memory_space=pltpu.HBM)] * 2,
        out_shape=[jax.ShapeDtypeStruct(shape, F32) for shape in shapes],
        scratch_shapes=[pltpu.VMEM(shares.shape, BF)]
        + [pltpu.VMEM(shape, F32) for shape in shapes]
        + [pltpu.SemaphoreType.DMA((jobs,))] * 2,
        compiler_params=params(),
        name="weight_spread",
    )(shares)


def exchange(array):
    return lax.all_to_all(array, AXES, split_axis=0, concat_axis=0, tiled=True)


def per_device(fields_in, lon_operator, w_in, w_out, inverses, cotangent):
    lat_tiles = lax.axis_size("lat")
    lon_tiles = lax.axis_size("lon")
    devices = lat_tiles * lon_tiles
    field_dev, _, grid_lon, grid_lat = fields_in.shape
    all_fields, all_levels, columns = cotangent.shape[2:]
    neurons, values = w_in.shape
    tile_lon = grid_lon // lon_tiles

    leaving = forward(
        fields_in.reshape(field_dev, grid_lon, grid_lat), lon_operator, lat_tiles, lon_tiles, tile_lon
    )
    arrived = exchange(leaving.reshape((devices,) + leaving.shape[2:]))

    matrix = inverses.reshape(all_levels, all_levels, columns)
    w_half = 0.5 * w_in
    grad_mixed = grad_mixed_of(matrix, cotangent.reshape(values, columns))

    going, cols = network(arrived, grad_mixed, w_half, w_out, lat_tiles)
    returned = exchange(going)

    diffused = diffused_of(cols, w_half, w_out, matrix, all_fields)

    shares = exchange(weight_sum(returned, diffused))
    grad_fields = adjoint(
        returned.reshape((lat_tiles, lon_tiles) + returned.shape[1:]), lon_operator, field_dev, grid_lat
    )
    grad_in, grad_out = weight_spread(shares, neurons, values)
    return (
        diffused.reshape(1, 1, all_fields, all_levels, columns),
        grad_fields.reshape(field_dev, 1, grid_lon, grid_lat),
        grad_in,
        grad_out,
    )


def solution(mesh):
    in_specs = (
        P("lat", "lon", None, None),
        P(),
        P(),
        P(),
        P("lat", "lon", None, None, None),
        P("lat", "lon", None, None, None),
    )
    out_specs = (P("lat", "lon", None, None, None), P("lat", "lon", None, None), P(), P())
    return jax.shard_map(
        per_device, mesh=mesh, in_specs=in_specs, out_specs=out_specs, check_vma=False
    )
```

```python
import functools

import jax
import jax.numpy as jnp
from jax import lax
from jax.experimental import pallas as pl
from jax.experimental.pallas import tpu as pltpu
from jax.sharding import PartitionSpec as P

KAPPA = 0.2
AXES = ("lat", "lon")
BF = jnp.bfloat16
F32 = jnp.float32
LANES = 128
QROWS = 8


def params(mebibytes=60):
    return pltpu.CompilerParams(vmem_limit_bytes=mebibytes * 1024 * 1024)


def in_vmem(x):
    return pltpu.with_memory_space_constraint(x, pltpu.VMEM)


def in_hbm(x):
    return pltpu.with_memory_space_constraint(x, pltpu.HBM)


def cost(flops, nbytes, trans=0):
    return pl.CostEstimate(flops=int(flops), bytes_accessed=int(nbytes), transcendentals=int(trans))


def dot(a, b, dims=(1, 0)):
    return lax.dot_general(a, b, (((dims[0],), (dims[1],)), ((), ())), preferred_element_type=F32)


def spread(wide):
    size = wide.shape[1]
    lane = lax.broadcasted_iota(jnp.int32, wide.shape, 1)
    before = jnp.where(lane == 0, 0.0, pltpu.roll(wide, 1, 1))
    after = jnp.where(lane == size - 1, 0.0, pltpu.roll(wide, size - 1, 1))
    return (1.0 - 2.0 * KAPPA) * wide + KAPPA * (after + before)


def forward_kernel(v_hbm, op_hbm, out_hbm, v_ref, op_ref, out_ref, v_sem, op_sem, out_sem):
    fields = v_ref.shape[0]
    blocks = op_ref.shape[0]
    block = op_ref.shape[2]
    tiles, _, chunks, rows, _ = out_ref.shape
    tile_lon = chunks * QROWS
    per_block = block // tile_lon

    def fetch_op(i):
        return pltpu.make_async_copy(op_hbm.at[:, pl.ds(i * block, block)], op_ref.at[i], op_sem.at[i])

    def fetch_v(f):
        return pltpu.make_async_copy(v_hbm.at[f], v_ref.at[f], v_sem.at[f])

    def store(i):
        part = pl.ds(i * per_block, per_block)
        return pltpu.make_async_copy(out_ref.at[:, part], out_hbm.at[:, part], out_sem.at[i])

    fetch_op(0).start()
    for f in range(fields):
        fetch_v(f).start()
    for i in range(1, blocks):
        fetch_op(i).start()
    def step(i, carry):
        fetch_op(i).wait()

        @pl.when(i == 0)
        def _():
            for f in range(fields):
                fetch_v(f).wait()

        rows_here = pl.ds(pl.multiple_of(i * block, block), block)
        done = []
        for f in range(fields):
            along = dot(op_ref[i], v_ref[f], (0, 0))
            wide = v_ref[f, rows_here, :].astype(F32)
            done.append(along + spread(wide))
        for a in range(tiles):
            parts = [
                d[:, a * LANES : (a + 1) * LANES].reshape(per_block, chunks, 1, QROWS, LANES)
                for d in done
            ]
            joined = jnp.concatenate(parts, axis=2).reshape(per_block, chunks, rows, LANES)
            out_ref[a, pl.ds(i * per_block, per_block)] = joined.astype(BF)
        store(i).start()
        return carry

    lax.fori_loop(0, blocks, step, 0)
    for i in range(blocks):
        store(i).wait()


def forward(fields_in, operator, lat_tiles, lon_tiles, tile_lon):
    fields, grid_lon, grid_lat = fields_in.shape
    chunks = tile_lon // QROWS
    block = 256
    blocks = grid_lon // block
    out_shape = (lat_tiles, lon_tiles, chunks, fields * QROWS, LANES)
    return pl.pallas_call(
        forward_kernel,
        in_specs=[pl.BlockSpec(memory_space=pltpu.HBM)] * 2,
        out_specs=pl.BlockSpec(memory_space=pltpu.HBM),
        out_shape=pltpu.HBM(out_shape, BF),
        scratch_shapes=[
            pltpu.VMEM(fields_in.shape, BF),
            pltpu.VMEM((blocks, grid_lon, block), BF),
            pltpu.VMEM(out_shape, BF),
            pltpu.SemaphoreType.DMA((fields,)),
            pltpu.SemaphoreType.DMA((blocks,)),
            pltpu.SemaphoreType.DMA((blocks,)),
        ],
        compiler_params=params(),
        cost_estimate=cost(2 * fields * grid_lon * grid_lon * grid_lat, 6 << 20),
        name="forward_dynamics",
    )(in_hbm(fields_in), in_hbm(operator))


def grad_mixed_kernel(inv_ref, cot_ref, out_ref, wide):
    levels = inv_ref.shape[0]
    fields = cot_ref.shape[0] // levels
    wide[...] = cot_ref[...].astype(F32)

    def tile(t, carry):
        lanes = pl.ds(pl.multiple_of(t * LANES, LANES), LANES)
        acc = [None] * fields
        for l in range(levels):
            matrix = inv_ref[l, :, lanes].astype(F32)
            for f in range(fields):
                term = matrix * wide[pl.ds(f * levels + l, 1), lanes]
                acc[f] = term if acc[f] is None else acc[f] + term
        for f in range(fields):
            out_ref[f * levels : (f + 1) * levels, lanes] = acc[f].astype(BF)
        return carry

    lax.fori_loop(0, inv_ref.shape[2] // LANES, tile, 0)


def grad_mixed_of(matrix, incoming):
    levels, _, columns = matrix.shape
    values = incoming.shape[0]
    chunk = 512
    return pl.pallas_call(
        grad_mixed_kernel,
        grid=(columns // chunk,),
        in_specs=[
            pl.BlockSpec((levels, levels, chunk), lambda i: (0, 0, i)),
            pl.BlockSpec((values, chunk), lambda i: (0, i)),
        ],
        out_specs=pl.BlockSpec((values, chunk), lambda i: (0, i)),
        out_shape=pltpu.HBM((values, columns), BF),
        scratch_shapes=[pltpu.VMEM((values, chunk), F32)],
        compiler_params=params(40),
        cost_estimate=cost(2 * values * levels * columns, 16 << 20),
        name="grad_mixed",
    )(in_hbm(matrix), in_hbm(incoming))


def network_kernel(
    arrived, gm_hbm, w_half, w_out,
    leaving_hbm, cols_hbm,
    gm, leaving, cols, act, grad_pre, wide_in, wide_out, acc_in, acc_out, gm_sem, out_sem, *, tiles,
):
    sources, steps, rows, _ = arrived.shape
    fields = rows // QROWS
    group = sources // tiles
    chunk = QROWS * LANES

    def fetch(i):
        return pltpu.make_async_copy(gm_hbm.at[:, pl.ds(i * chunk, chunk)], gm.at[i], gm_sem.at[i])

    def store_leaving(i):
        return pltpu.make_async_copy(leaving.at[i], leaving_hbm.at[:, i], out_sem.at[0, i])

    def store_cols(i):
        return pltpu.make_async_copy(
            cols.at[i], cols_hbm.at[:, pl.ds(i * chunk, chunk)], out_sem.at[1, i]
        )

    for i in range(steps):
        fetch(i).start()
    acc_in[...] = jnp.zeros_like(acc_in)
    acc_out[...] = jnp.zeros_like(acc_out)
    def step(i, carry):
        wide_in[...] = arrived[:, i].astype(F32).reshape(sources * rows, LANES)
        for q in range(QROWS):
            by_field = [
                wide_in[pl.ds(f * QROWS + q, sources, stride=rows), :] for f in range(fields)
            ]
            parts = [
                by_field[f][a * group : (a + 1) * group] for a in range(tiles) for f in range(fields)
            ]
            cols[i, :, q * LANES : (q + 1) * LANES] = jnp.concatenate(parts, axis=0).astype(BF)
        fetch(i).wait()
        half = dot(w_half[...], cols[i])
        turn = jnp.tanh(half)
        value = half + half * turn
        act[...] = value.astype(BF)
        slope = 1.0 + (turn + value) - turn * value
        grad_pre[...] = (dot(w_out[...], gm[i], (0, 0)) * slope).astype(BF)
        grad_cols = gm[i].astype(F32) + dot(w_half[...], grad_pre[...], (0, 0))
        acc_in[...] += dot(grad_pre[...], cols[i], (1, 1))
        acc_out[...] += dot(act[...], gm[i], (1, 1))
        for q in range(QROWS):
            piece = grad_cols[:, q * LANES : (q + 1) * LANES]
            for f in range(fields):
                parts = [
                    piece[(a * fields + f) * group : (a * fields + f + 1) * group]
                    for a in range(tiles)
                ]
                wide_out[pl.ds(f * QROWS + q, sources, stride=rows), :] = jnp.concatenate(
                    parts, axis=0
                )
        leaving[i] = wide_out[...].reshape(sources, rows, LANES).astype(BF)
        store_cols(i).start()
        store_leaving(i).start()
        return carry

    lax.fori_loop(0, steps, step, 0)
    total_in = 0.5 * acc_in[...]
    total_out = acc_out[...]
    place = 0
    for total in (total_in, total_out):
        height, breadth = total.shape
        for j in range(breadth // LANES):
            count = height // rows
            part = total[:, j * LANES : (j + 1) * LANES].reshape(count, rows, LANES)
            leaving[steps, place : place + count] = part.astype(BF)
            place += count
    store_leaving(steps).start()
    for i in range(steps):
        store_cols(i).wait()
        store_leaving(i).wait()
    store_leaving(steps).wait()


def network(arrived, grad_mixed, w_half, w_out, tiles):
    sources, steps, rows, _ = arrived.shape
    values, columns = grad_mixed.shape
    neurons = w_half.shape[0]
    chunk = columns // steps
    return pl.pallas_call(
        functools.partial(network_kernel, tiles=tiles),
        in_specs=[
            pl.BlockSpec(memory_space=pltpu.VMEM),
            pl.BlockSpec(memory_space=pltpu.HBM),
            pl.BlockSpec(memory_space=pltpu.VMEM),
            pl.BlockSpec(memory_space=pltpu.VMEM),
        ],
        out_specs=[pl.BlockSpec(memory_space=pltpu.HBM)] * 2,
        out_shape=[
            pltpu.HBM((sources, steps + 1, rows, LANES), BF),
            pltpu.HBM((values, columns), BF),
        ],
        scratch_shapes=[
            pltpu.VMEM((steps, values, chunk), BF),
            pltpu.VMEM((steps + 1, sources, rows, LANES), BF),
            pltpu.VMEM((steps, values, chunk), BF),
            pltpu.VMEM((neurons, chunk), BF),
            pltpu.VMEM((neurons, chunk), BF),
            pltpu.VMEM((sources * rows, LANES), F32),
            pltpu.VMEM((sources * rows, LANES), F32),
            pltpu.VMEM((neurons, values), F32),
            pltpu.VMEM((neurons, values), F32),
            pltpu.SemaphoreType.DMA((steps,)),
            pltpu.SemaphoreType.DMA((2, steps + 1)),
        ],
        compiler_params=params(40),
        cost_estimate=cost(8 * neurons * values * columns, 14 << 20, neurons * columns),
        name="column_network",
    )(in_vmem(arrived), in_hbm(grad_mixed), in_vmem(w_half), in_vmem(w_out))


def diffused_kernel(cols_ref, w_half_ref, w_out_ref, inv_ref, out_ref, mixed, flat):
    fields, levels = out_ref.shape[0], out_ref.shape[1]
    half = dot(w_half_ref[...], cols_ref[...])
    act = (half + half * jnp.tanh(half)).astype(BF)
    total = cols_ref[...].astype(F32) + dot(w_out_ref[...], act)
    mixed[...] = total.astype(BF).astype(F32)

    def tile(t, carry):
        lanes = pl.ds(pl.multiple_of(t * LANES, LANES), LANES)
        flat[...] = inv_ref[:, :, lanes].astype(F32).reshape(levels * levels, LANES)
        acc = [None] * fields
        for m in range(levels):
            matrix = flat[pl.ds(m, levels, stride=levels), :]
            for f in range(fields):
                term = matrix * mixed[pl.ds(f * levels + m, 1), lanes]
                acc[f] = term if acc[f] is None else acc[f] + term
        for f in range(fields):
            out_ref[f, :, lanes] = acc[f]
        return carry

    lax.fori_loop(0, inv_ref.shape[2] // LANES, tile, 0)


def diffused_of(cols, w_half, w_out, matrix, fields):
    levels, _, columns = matrix.shape
    values, neurons = w_out.shape
    chunk = 512
    return pl.pallas_call(
        diffused_kernel,
        grid=(columns // chunk,),
        in_specs=[
            pl.BlockSpec((values, chunk), lambda i: (0, i)),
            pl.BlockSpec((neurons, values), lambda i: (0, 0)),
            pl.BlockSpec((values, neurons), lambda i: (0, 0)),
            pl.BlockSpec((levels, levels, chunk), lambda i: (0, 0, i)),
        ],
        out_specs=pl.BlockSpec((fields, levels, chunk), lambda i: (0, 0, i)),
        out_shape=jax.ShapeDtypeStruct((fields, levels, columns), F32),
        scratch_shapes=[
            pltpu.VMEM((values, chunk), F32),
            pltpu.VMEM((levels * levels, LANES), F32),
        ],
        compiler_params=params(),
        cost_estimate=cost(2 * values * (levels + 2 * neurons) * columns, 16 << 20),
        name="diffused",
    )(in_hbm(cols), w_half, w_out, in_hbm(matrix))


def adjoint_kernel(back, op_hbm, out_hbm, op_ref, grid_ref, out_ref, op_sem, out_sem):
    fields = out_ref.shape[0]
    tiles, lon_tiles = back.shape[:2]
    grid_lon = grid_ref.shape[1]
    chunks = grid_lon // (lon_tiles * QROWS)
    block = 256
    blocks = grid_lon // block

    def fetch_op(i):
        part = pl.ds(i * block, block)
        return pltpu.make_async_copy(op_hbm.at[part], op_ref.at[part], op_sem.at[i])

    def store(f, i):
        part = pl.ds(i * block, block)
        return pltpu.make_async_copy(out_ref.at[f, part], out_hbm.at[f, part], out_sem.at[f, i])

    for i in range(blocks):
        fetch_op(i).start()
    for a in range(tiles):
        wide = back[a, :, :chunks].astype(F32).reshape(lon_tiles * chunks, fields, QROWS, LANES)
        for f in range(fields):
            grid_ref[f, :, a * LANES : (a + 1) * LANES] = (
                wide[:, f].reshape(grid_lon, LANES).astype(BF)
            )
    def step(i, carry):
        fetch_op(i).wait()
        part = pl.ds(pl.multiple_of(i * block, block), block)
        for f in range(fields):
            along = dot(op_ref[part, :], grid_ref[f])
            wide = grid_ref[f, part, :].astype(F32)
            out_ref[f, part, :] = along + spread(wide)
            store(f, i).start()
        return carry

    lax.fori_loop(0, blocks, step, 0)
    for i in range(blocks):
        for f in range(fields):
            store(f, i).wait()


def adjoint(returned, operator, fields, grid_lat):
    grid_lon = operator.shape[0]
    blocks = grid_lon // 256
    return pl.pallas_call(
        adjoint_kernel,
        in_specs=[pl.BlockSpec(memory_space=pltpu.VMEM), pl.BlockSpec(memory_space=pltpu.HBM)],
        out_specs=pl.BlockSpec(memory_space=pltpu.HBM),
        out_shape=jax.ShapeDtypeStruct((fields, grid_lon, grid_lat), F32),
        scratch_shapes=[
            pltpu.VMEM(operator.shape, BF),
            pltpu.VMEM((fields, grid_lon, grid_lat), BF),
            pltpu.VMEM((fields, grid_lon, grid_lat), F32),
            pltpu.SemaphoreType.DMA((blocks,)),
            pltpu.SemaphoreType.DMA((fields, blocks)),
        ],
        compiler_params=params(48),
        cost_estimate=cost(2 * fields * grid_lon * grid_lon * grid_lat, 8 << 20),
        name="adjoint_dynamics",
    )(in_vmem(returned), in_hbm(operator))


def weight_sum_kernel(returned, _, out_hbm, out_ref, out_sem):
    last = returned.shape[1] - 1
    total = jnp.sum(returned[:, last].astype(F32), axis=0, keepdims=True)
    out_ref[...] = jnp.broadcast_to(total.astype(BF), out_ref.shape)
    store = pltpu.make_async_copy(out_ref, out_hbm, out_sem)
    store.start()
    store.wait()


def weight_sum(returned, after):
    sources, _, rows, _ = returned.shape
    shape = (sources, rows, LANES)
    return pl.pallas_call(
        weight_sum_kernel,
        in_specs=[pl.BlockSpec(memory_space=pltpu.VMEM), pl.BlockSpec(memory_space=pltpu.HBM)],
        out_specs=pl.BlockSpec(memory_space=pltpu.HBM),
        out_shape=pltpu.HBM(shape, BF),
        scratch_shapes=[pltpu.VMEM(shape, BF), pltpu.SemaphoreType.DMA],
        compiler_params=params(48),
        cost_estimate=cost(sources * rows * LANES, 1 << 20),
        name="weight_sum",
    )(in_vmem(returned), in_hbm(after))


def weight_spread_kernel(shares, in_hbm, out_hbm, in_ref, out_ref, out_sem):
    rows = shares.shape[1]
    height, breadth = in_ref.shape
    count = height // rows
    each = breadth // LANES
    jobs = 2 * each

    def store(k):
        part = pl.ds((k % each) * LANES, LANES)
        if k < each:
            return pltpu.make_async_copy(in_ref.at[:, part], in_hbm.at[:, part], out_sem.at[k])
        return pltpu.make_async_copy(out_ref.at[part], out_hbm.at[part], out_sem.at[k])

    for k in range(jobs):
        wide = shares[k * count : (k + 1) * count].astype(F32).reshape(height, LANES)
        part = slice((k % each) * LANES, (k % each + 1) * LANES)
        if k < each:
            in_ref[:, part] = wide
        else:
            out_ref[part, :] = wide.T
        store(k).start()
    for k in range(jobs):
        store(k).wait()


def weight_spread(shares, neurons, values):
    shapes = [(neurons, values), (values, neurons)]
    jobs = 2 * (values // LANES)
    return pl.pallas_call(
        weight_spread_kernel,
        in_specs=[pl.BlockSpec(memory_space=pltpu.VMEM)],
        out_specs=[pl.BlockSpec(memory_space=pltpu.HBM)] * 2,
        out_shape=[jax.ShapeDtypeStruct(shape, F32) for shape in shapes],
        scratch_shapes=[pltpu.VMEM(shape, F32) for shape in shapes]
        + [pltpu.SemaphoreType.DMA((jobs,))],
        compiler_params=params(48),
        name="weight_spread",
    )(in_vmem(shares))


def exchange(array):
    return lax.all_to_all(array, AXES, split_axis=0, concat_axis=0, tiled=True)


def per_device(fields_in, lon_operator, w_in, w_out, inverses, cotangent):
    lat_tiles = lax.axis_size("lat")
    lon_tiles = lax.axis_size("lon")
    devices = lat_tiles * lon_tiles
    field_dev, _, grid_lon, grid_lat = fields_in.shape
    all_fields, all_levels, columns = cotangent.shape[2:]
    neurons, values = w_in.shape
    tile_lon = grid_lon // lon_tiles

    leaving = forward(
        fields_in.reshape(field_dev, grid_lon, grid_lat), lon_operator, lat_tiles, lon_tiles, tile_lon
    )
    arrived = exchange(leaving.reshape((devices,) + leaving.shape[2:]))

    matrix = inverses.reshape(all_levels, all_levels, columns)
    w_half = 0.5 * w_in
    grad_mixed = grad_mixed_of(matrix, cotangent.reshape(values, columns))

    going, cols = network(arrived, grad_mixed, w_half, w_out, lat_tiles)
    returned = exchange(going)

    diffused = diffused_of(cols, w_half, w_out, matrix, all_fields)

    shares = exchange(weight_sum(returned, diffused))
    grad_fields = adjoint(
        returned.reshape((lat_tiles, lon_tiles) + returned.shape[1:]), lon_operator, field_dev, grid_lat
    )
    grad_in, grad_out = weight_spread(shares, neurons, values)
    return (
        diffused.reshape(1, 1, all_fields, all_levels, columns),
        grad_fields.reshape(field_dev, 1, grid_lon, grid_lat),
        grad_in,
        grad_out,
    )


def solution(mesh):
    in_specs = (
        P("lat", "lon", None, None),
        P(),
        P(),
        P(),
        P("lat", "lon", None, None, None),
        P("lat", "lon", None, None, None),
    )
    out_specs = (P("lat", "lon", None, None, None), P("lat", "lon", None, None), P(), P())
    return jax.shard_map(
        per_device, mesh=mesh, in_specs=in_specs, out_specs=out_specs, check_vma=False
    )
```

```python
import functools

import jax
import jax.numpy as jnp
from jax import lax
from jax.experimental import pallas as pl
from jax.experimental.pallas import tpu as pltpu
from jax.sharding import PartitionSpec as P

KAPPA = 0.2
AXES = ("lat", "lon")
BF = jnp.bfloat16
F32 = jnp.float32
LANES = 128
QROWS = 8
PAD = 8


def params(mebibytes=60):
    return pltpu.CompilerParams(vmem_limit_bytes=mebibytes * 1024 * 1024)


def in_vmem(x):
    return pltpu.with_memory_space_constraint(x, pltpu.VMEM)


def in_hbm(x):
    return pltpu.with_memory_space_constraint(x, pltpu.HBM)


def cost(flops, nbytes, trans=0):
    return pl.CostEstimate(flops=int(flops), bytes_accessed=int(nbytes), transcendentals=int(trans))


def dot(a, b, dims=(1, 0)):
    return lax.dot_general(a, b, (((dims[0],), (dims[1],)), ((), ())), preferred_element_type=F32)


def spread(wide):
    size = wide.shape[1]
    lane = lax.broadcasted_iota(jnp.int32, wide.shape, 1)
    before = jnp.where(lane == 0, 0.0, pltpu.roll(wide, 1, 1))
    after = jnp.where(lane == size - 1, 0.0, pltpu.roll(wide, size - 1, 1))
    return (1.0 - 2.0 * KAPPA) * wide + KAPPA * (after + before)


def forward_kernel(v_hbm, op_hbm, out_hbm, v_ref, op_ref, out_ref, v_sem, op_sem, out_sem):
    fields = v_ref.shape[0]
    blocks = op_ref.shape[0]
    block = op_ref.shape[2]
    tiles, _, chunks, rows, _ = out_ref.shape
    tile_lon = chunks * QROWS
    per_block = block // tile_lon

    def fetch_op(i):
        return pltpu.make_async_copy(op_hbm.at[:, pl.ds(i * block, block)], op_ref.at[i], op_sem.at[i])

    def fetch_v(f):
        return pltpu.make_async_copy(v_hbm.at[f], v_ref.at[f], v_sem.at[f])

    def store(i):
        part = pl.ds(i * per_block, per_block)
        return pltpu.make_async_copy(out_ref.at[:, part], out_hbm.at[:, part], out_sem.at[i])

    fetch_op(0).start()
    for f in range(fields):
        fetch_v(f).start()
    for i in range(1, blocks):
        fetch_op(i).start()
    def step(i, carry):
        fetch_op(i).wait()

        @pl.when(i == 0)
        def _():
            for f in range(fields):
                fetch_v(f).wait()

        rows_here = pl.ds(pl.multiple_of(i * block, block), block)
        done = []
        for f in range(fields):
            along = dot(op_ref[i], v_ref[f], (0, 0))
            wide = v_ref[f, rows_here, :].astype(F32)
            done.append(along + spread(wide))
        for a in range(tiles):
            parts = [
                d[:, a * LANES : (a + 1) * LANES].reshape(per_block, chunks, 1, QROWS, LANES)
                for d in done
            ]
            joined = jnp.concatenate(parts, axis=2).reshape(per_block, chunks, rows, LANES)
            out_ref[a, pl.ds(i * per_block, per_block)] = joined.astype(BF)
        store(i).start()
        return carry

    lax.fori_loop(0, blocks, step, 0)
    for i in range(blocks):
        store(i).wait()


def forward(fields_in, operator, lat_tiles, lon_tiles, tile_lon):
    fields, grid_lon, grid_lat = fields_in.shape
    chunks = tile_lon // QROWS
    block = 256
    blocks = grid_lon // block
    out_shape = (lat_tiles, lon_tiles, chunks, fields * QROWS, LANES)
    return pl.pallas_call(
        forward_kernel,
        in_specs=[pl.BlockSpec(memory_space=pltpu.HBM)] * 2,
        out_specs=pl.BlockSpec(memory_space=pltpu.HBM),
        out_shape=pltpu.HBM(out_shape, BF),
        scratch_shapes=[
            pltpu.VMEM(fields_in.shape, BF),
            pltpu.VMEM((blocks, grid_lon, block), BF),
            pltpu.VMEM(out_shape, BF),
            pltpu.SemaphoreType.DMA((fields,)),
            pltpu.SemaphoreType.DMA((blocks,)),
            pltpu.SemaphoreType.DMA((blocks,)),
        ],
        compiler_params=params(),
        cost_estimate=cost(2 * fields * grid_lon * grid_lon * grid_lat, 6 << 20),
        name="forward_dynamics",
    )(in_hbm(fields_in), in_hbm(operator))


def grad_mixed_kernel(inv_ref, cot_ref, out_ref, wide):
    levels = inv_ref.shape[0]
    fields = cot_ref.shape[0] // levels
    wide[...] = cot_ref[...].astype(F32)

    def tile(t, carry):
        lanes = pl.ds(pl.multiple_of(t * LANES, LANES), LANES)
        acc = [None] * fields
        for l in range(levels):
            matrix = inv_ref[l, :, lanes].astype(F32)
            for f in range(fields):
                term = matrix * wide[pl.ds(f * levels + l, 1), lanes]
                acc[f] = term if acc[f] is None else acc[f] + term
        for f in range(fields):
            out_ref[f * levels : (f + 1) * levels, lanes] = acc[f].astype(BF)
        return carry

    lax.fori_loop(0, inv_ref.shape[2] // LANES, tile, 0)


def grad_mixed_of(matrix, incoming):
    levels, _, columns = matrix.shape
    values = incoming.shape[0]
    chunk = 512
    return pl.pallas_call(
        grad_mixed_kernel,
        grid=(columns // chunk,),
        in_specs=[
            pl.BlockSpec((levels, levels, chunk), lambda i: (0, 0, i)),
            pl.BlockSpec((values, chunk), lambda i: (0, i)),
        ],
        out_specs=pl.BlockSpec((values, chunk), lambda i: (0, i)),
        out_shape=pltpu.HBM((values, columns), BF),
        scratch_shapes=[pltpu.VMEM((values, chunk), F32)],
        compiler_params=params(40),
        cost_estimate=cost(2 * values * levels * columns, 16 << 20),
        name="grad_mixed",
    )(in_hbm(matrix), in_hbm(incoming))


def network_kernel(
    arrived, gm_hbm, w_half, w_out,
    leaving_hbm, cols_hbm,
    gm, leaving, cols, act, grad_pre, wide_in, wide_out, acc_in, acc_out, gm_sem, out_sem, *, tiles,
):
    sources, steps, rows, _ = arrived.shape
    fields = rows // QROWS
    group = sources // tiles
    chunk = QROWS * LANES
    pitch = wide_in.shape[0] // (sources + 1)

    def fetch(i):
        return pltpu.make_async_copy(gm_hbm.at[:, pl.ds(i * chunk, chunk)], gm.at[i], gm_sem.at[i])

    def store_leaving(i):
        return pltpu.make_async_copy(leaving.at[i], leaving_hbm.at[:, i], out_sem.at[0, i])

    def store_cols(i):
        return pltpu.make_async_copy(
            cols.at[i], cols_hbm.at[:, pl.ds(i * chunk, chunk)], out_sem.at[1, i]
        )

    for i in range(steps):
        fetch(i).start()
    acc_in[...] = jnp.zeros_like(acc_in)
    acc_out[...] = jnp.zeros_like(acc_out)

    def step(i, carry):
        for s in range(sources):
            wide_in[s * pitch : s * pitch + rows, :] = arrived[s, i].astype(F32)
        for q in range(QROWS):
            by_field = [
                wide_in[pl.ds(f * QROWS + q, sources, stride=pitch), :] for f in range(fields)
            ]
            parts = [
                by_field[f][a * group : (a + 1) * group] for a in range(tiles) for f in range(fields)
            ]
            cols[i, :, q * LANES : (q + 1) * LANES] = jnp.concatenate(parts, axis=0).astype(BF)
        half = dot(w_half[...], cols[i])
        turn = jnp.tanh(half)
        value = half + half * turn
        act[...] = value.astype(BF)
        fetch(i).wait()
        slope = 1.0 + (turn + value) - turn * value
        grad_pre[...] = (dot(w_out[...], gm[i], (0, 0)) * slope).astype(BF)
        acc_in[...] += dot(grad_pre[...], cols[i], (1, 1))
        acc_out[...] += dot(act[...], gm[i], (1, 1))
        grad_cols = gm[i].astype(F32) + dot(w_half[...], grad_pre[...], (0, 0))
        for q in range(QROWS):
            piece = grad_cols[:, q * LANES : (q + 1) * LANES]
            for f in range(fields):
                parts = [
                    piece[(a * fields + f) * group : (a * fields + f + 1) * group]
                    for a in range(tiles)
                ]
                wide_out[pl.ds(f * QROWS + q, sources, stride=pitch), :] = jnp.concatenate(
                    parts, axis=0
                )
        for s in range(sources):
            leaving[i, s] = wide_out[s * pitch : s * pitch + rows, :].astype(BF)
        store_cols(i).start()
        store_leaving(i).start()
        return carry

    lax.fori_loop(0, steps, step, 0)
    total_in = 0.5 * acc_in[...]
    total_out = acc_out[...]
    place = 0
    for total in (total_in, total_out):
        height, breadth = total.shape
        for j in range(breadth // LANES):
            count = height // rows
            part = total[:, j * LANES : (j + 1) * LANES].reshape(count, rows, LANES)
            leaving[steps, place : place + count] = part.astype(BF)
            place += count
    store_leaving(steps).start()
    for i in range(steps):
        store_cols(i).wait()
        store_leaving(i).wait()
    store_leaving(steps).wait()


def network(arrived, grad_mixed, w_half, w_out, tiles):
    sources, steps, rows, _ = arrived.shape
    values, columns = grad_mixed.shape
    neurons = w_half.shape[0]
    chunk = columns // steps
    return pl.pallas_call(
        functools.partial(network_kernel, tiles=tiles),
        in_specs=[
            pl.BlockSpec(memory_space=pltpu.VMEM),
            pl.BlockSpec(memory_space=pltpu.HBM),
            pl.BlockSpec(memory_space=pltpu.VMEM),
            pl.BlockSpec(memory_space=pltpu.VMEM),
        ],
        out_specs=[pl.BlockSpec(memory_space=pltpu.HBM)] * 2,
        out_shape=[
            pltpu.HBM((sources, steps + 1, rows, LANES), BF),
            pltpu.HBM((values, columns), BF),
        ],
        scratch_shapes=[
            pltpu.VMEM((steps, values, chunk), BF),
            pltpu.VMEM((steps + 1, sources, rows, LANES), BF),
            pltpu.VMEM((steps, values, chunk), BF),
            pltpu.VMEM((neurons, chunk), BF),
            pltpu.VMEM((neurons, chunk), BF),
            pltpu.VMEM(((sources + 1) * (rows + PAD), LANES), F32),
            pltpu.VMEM(((sources + 1) * (rows + PAD), LANES), F32),
            pltpu.VMEM((neurons, values), F32),
            pltpu.VMEM((neurons, values), F32),
            pltpu.SemaphoreType.DMA((steps,)),
            pltpu.SemaphoreType.DMA((2, steps + 1)),
        ],
        compiler_params=params(40),
        cost_estimate=cost(8 * neurons * values * columns, 14 << 20, neurons * columns),
        name="column_network",
    )(in_vmem(arrived), in_hbm(grad_mixed), in_vmem(w_half), in_vmem(w_out))


def diffused_kernel(cols_ref, w_half_ref, w_out_ref, inv_ref, out_ref, mixed, flat):
    fields, levels = out_ref.shape[0], out_ref.shape[1]
    half = dot(w_half_ref[...], cols_ref[...])
    act = (half + half * jnp.tanh(half)).astype(BF)
    total = cols_ref[...].astype(F32) + dot(w_out_ref[...], act)
    mixed[...] = total.astype(BF).astype(F32)

    def tile(t, carry):
        lanes = pl.ds(pl.multiple_of(t * LANES, LANES), LANES)
        flat[: levels * levels] = inv_ref[:, :, lanes].astype(F32).reshape(levels * levels, LANES)
        acc = [None] * fields
        for m in range(levels):
            matrix = flat[pl.ds(m, levels, stride=levels), :]
            for f in range(fields):
                term = matrix * mixed[pl.ds(f * levels + m, 1), lanes]
                acc[f] = term if acc[f] is None else acc[f] + term
        for f in range(fields):
            out_ref[f, :, lanes] = acc[f]
        return carry

    lax.fori_loop(0, inv_ref.shape[2] // LANES, tile, 0)


def diffused_of(cols, w_half, w_out, matrix, fields):
    levels, _, columns = matrix.shape
    values, neurons = w_out.shape
    chunk = 512
    return pl.pallas_call(
        diffused_kernel,
        grid=(columns // chunk,),
        in_specs=[
            pl.BlockSpec((values, chunk), lambda i: (0, i)),
            pl.BlockSpec((neurons, values), lambda i: (0, 0)),
            pl.BlockSpec((values, neurons), lambda i: (0, 0)),
            pl.BlockSpec((levels, levels, chunk), lambda i: (0, 0, i)),
        ],
        out_specs=pl.BlockSpec((fields, levels, chunk), lambda i: (0, 0, i)),
        out_shape=jax.ShapeDtypeStruct((fields, levels, columns), F32),
        scratch_shapes=[
            pltpu.VMEM((values, chunk), F32),
            pltpu.VMEM(((levels + 1) * levels, LANES), F32),
        ],
        compiler_params=params(),
        cost_estimate=cost(2 * values * (levels + 2 * neurons) * columns, 16 << 20),
        name="diffused",
    )(in_hbm(cols), w_half, w_out, in_hbm(matrix))


def adjoint_kernel(back, op_hbm, out_hbm, op_ref, grid_ref, out_ref, op_sem, out_sem):
    fields = out_ref.shape[0]
    tiles, lon_tiles = back.shape[:2]
    grid_lon = grid_ref.shape[1]
    chunks = grid_lon // (lon_tiles * QROWS)
    block = 256
    blocks = grid_lon // block

    def fetch_op(i):
        part = pl.ds(i * block, block)
        return pltpu.make_async_copy(op_hbm.at[part], op_ref.at[part], op_sem.at[i])

    def store(f, i):
        part = pl.ds(i * block, block)
        return pltpu.make_async_copy(out_ref.at[f, part], out_hbm.at[f, part], out_sem.at[f, i])

    for i in range(blocks):
        fetch_op(i).start()
    for a in range(tiles):
        wide = back[a, :, :chunks].astype(F32).reshape(lon_tiles * chunks, fields, QROWS, LANES)
        for f in range(fields):
            grid_ref[f, :, a * LANES : (a + 1) * LANES] = (
                wide[:, f].reshape(grid_lon, LANES).astype(BF)
            )
    def step(i, carry):
        fetch_op(i).wait()
        part = pl.ds(pl.multiple_of(i * block, block), block)
        for f in range(fields):
            along = dot(op_ref[part, :], grid_ref[f])
            wide = grid_ref[f, part, :].astype(F32)
            out_ref[f, part, :] = along + spread(wide)
            store(f, i).start()
        return carry

    lax.fori_loop(0, blocks, step, 0)
    for i in range(blocks):
        for f in range(fields):
            store(f, i).wait()


def adjoint(returned, operator, fields, grid_lat):
    grid_lon = operator.shape[0]
    blocks = grid_lon // 256
    return pl.pallas_call(
        adjoint_kernel,
        in_specs=[pl.BlockSpec(memory_space=pltpu.VMEM), pl.BlockSpec(memory_space=pltpu.HBM)],
        out_specs=pl.BlockSpec(memory_space=pltpu.HBM),
        out_shape=jax.ShapeDtypeStruct((fields, grid_lon, grid_lat), F32),
        scratch_shapes=[
            pltpu.VMEM(operator.shape, BF),
            pltpu.VMEM((fields, grid_lon, grid_lat), BF),
            pltpu.VMEM((fields, grid_lon, grid_lat), F32),
            pltpu.SemaphoreType.DMA((blocks,)),
            pltpu.SemaphoreType.DMA((fields, blocks)),
        ],
        compiler_params=params(48),
        cost_estimate=cost(2 * fields * grid_lon * grid_lon * grid_lat, 8 << 20),
        name="adjoint_dynamics",
    )(in_vmem(returned), in_hbm(operator))


def weight_sum_kernel(returned, _, out_hbm, out_ref, out_sem):
    last = returned.shape[1] - 1
    total = jnp.sum(returned[:, last].astype(F32), axis=0, keepdims=True)
    out_ref[...] = jnp.broadcast_to(total.astype(BF), out_ref.shape)
    store = pltpu.make_async_copy(out_ref, out_hbm, out_sem)
    store.start()
    store.wait()


def weight_sum(returned, after):
    sources, _, rows, _ = returned.shape
    shape = (sources, rows, LANES)
    return pl.pallas_call(
        weight_sum_kernel,
        in_specs=[pl.BlockSpec(memory_space=pltpu.VMEM), pl.BlockSpec(memory_space=pltpu.HBM)],
        out_specs=pl.BlockSpec(memory_space=pltpu.HBM),
        out_shape=pltpu.HBM(shape, BF),
        scratch_shapes=[pltpu.VMEM(shape, BF), pltpu.SemaphoreType.DMA],
        compiler_params=params(48),
        cost_estimate=cost(sources * rows * LANES, 1 << 20),
        name="weight_sum",
    )(in_vmem(returned), in_hbm(after))


def weight_spread_kernel(shares, in_hbm, out_hbm, in_ref, out_ref, out_sem):
    rows = shares.shape[1]
    height, breadth = in_ref.shape
    count = height // rows
    each = breadth // LANES
    jobs = 2 * each

    def store(k):
        part = pl.ds((k % each) * LANES, LANES)
        if k < each:
            return pltpu.make_async_copy(in_ref.at[:, part], in_hbm.at[:, part], out_sem.at[k])
        return pltpu.make_async_copy(out_ref.at[part], out_hbm.at[part], out_sem.at[k])

    for k in range(jobs):
        wide = shares[k * count : (k + 1) * count].astype(F32).reshape(height, LANES)
        part = slice((k % each) * LANES, (k % each + 1) * LANES)
        if k < each:
            in_ref[:, part] = wide
        else:
            out_ref[part, :] = wide.T
        store(k).start()
    for k in range(jobs):
        store(k).wait()


def weight_spread(shares, neurons, values):
    shapes = [(neurons, values), (values, neurons)]
    jobs = 2 * (values // LANES)
    return pl.pallas_call(
        weight_spread_kernel,
        in_specs=[pl.BlockSpec(memory_space=pltpu.VMEM)],
        out_specs=[pl.BlockSpec(memory_space=pltpu.HBM)] * 2,
        out_shape=[jax.ShapeDtypeStruct(shape, F32) for shape in shapes],
        scratch_shapes=[pltpu.VMEM(shape, F32) for shape in shapes]
        + [pltpu.SemaphoreType.DMA((jobs,))],
        compiler_params=params(48),
        name="weight_spread",
    )(in_vmem(shares))


def exchange(array):
    return lax.all_to_all(array, AXES, split_axis=0, concat_axis=0, tiled=True)


def per_device(fields_in, lon_operator, w_in, w_out, inverses, cotangent):
    lat_tiles = lax.axis_size("lat")
    lon_tiles = lax.axis_size("lon")
    devices = lat_tiles * lon_tiles
    field_dev, _, grid_lon, grid_lat = fields_in.shape
    all_fields, all_levels, columns = cotangent.shape[2:]
    neurons, values = w_in.shape
    tile_lon = grid_lon // lon_tiles

    leaving = forward(
        fields_in.reshape(field_dev, grid_lon, grid_lat), lon_operator, lat_tiles, lon_tiles, tile_lon
    )
    arrived = exchange(leaving.reshape((devices,) + leaving.shape[2:]))

    matrix = inverses.reshape(all_levels, all_levels, columns)
    w_half = 0.5 * w_in
    grad_mixed = grad_mixed_of(matrix, cotangent.reshape(values, columns))

    going, cols = network(arrived, grad_mixed, w_half, w_out, lat_tiles)
    returned = exchange(going)

    diffused = diffused_of(cols, w_half, w_out, matrix, all_fields)

    shares = exchange(weight_sum(returned, diffused))
    grad_fields = adjoint(
        returned.reshape((lat_tiles, lon_tiles) + returned.shape[1:]), lon_operator, field_dev, grid_lat
    )
    grad_in, grad_out = weight_spread(shares, neurons, values)
    return (
        diffused.reshape(1, 1, all_fields, all_levels, columns),
        grad_fields.reshape(field_dev, 1, grid_lon, grid_lat),
        grad_in,
        grad_out,
    )


def solution(mesh):
    in_specs = (
        P("lat", "lon", None, None),
        P(),
        P(),
        P(),
        P("lat", "lon", None, None, None),
        P("lat", "lon", None, None, None),
    )
    out_specs = (P("lat", "lon", None, None, None), P("lat", "lon", None, None), P(), P())
    return jax.shard_map(
        per_device, mesh=mesh, in_specs=in_specs, out_specs=out_specs, check_vma=False
    )
```

```python
import functools

import jax
import jax.numpy as jnp
from jax import lax
from jax.experimental import pallas as pl
from jax.experimental.pallas import tpu as pltpu
from jax.sharding import PartitionSpec as P

KAPPA = 0.2
AXES = ("lat", "lon")
BF = jnp.bfloat16
F32 = jnp.float32
LANES = 128
QROWS = 8
PAD = 8


def params(mebibytes=60):
    return pltpu.CompilerParams(vmem_limit_bytes=mebibytes * 1024 * 1024)


def in_vmem(x):
    return pltpu.with_memory_space_constraint(x, pltpu.VMEM)


def in_hbm(x):
    return pltpu.with_memory_space_constraint(x, pltpu.HBM)


def cost(flops, nbytes, trans=0):
    return pl.CostEstimate(flops=int(flops), bytes_accessed=int(nbytes), transcendentals=int(trans))


def dot(a, b, dims=(1, 0)):
    return lax.dot_general(a, b, (((dims[0],), (dims[1],)), ((), ())), preferred_element_type=F32)


def stencil(size):
    row = lax.broadcasted_iota(jnp.int32, (size, size), 0)
    lane = lax.broadcasted_iota(jnp.int32, (size, size), 1)
    apart = jnp.abs(row - lane)
    return jnp.where(apart == 0, 1.0 / KAPPA - 2.0, jnp.where(apart == 1, 1.0, 0.0)).astype(BF)


def spread(wide):
    size = wide.shape[1]
    lane = lax.broadcasted_iota(jnp.int32, wide.shape, 1)
    before = jnp.where(lane == 0, 0.0, pltpu.roll(wide, 1, 1))
    after = jnp.where(lane == size - 1, 0.0, pltpu.roll(wide, size - 1, 1))
    return (1.0 - 2.0 * KAPPA) * wide + KAPPA * (after + before)


def forward_kernel(v_hbm, op_hbm, out_hbm, v_ref, op_ref, out_ref, near, side, v_sem, op_sem, out_sem):
    fields = v_ref.shape[0]
    blocks = op_ref.shape[0]
    block = op_ref.shape[2]
    tiles, _, chunks, rows, _ = out_ref.shape
    tile_lon = chunks * QROWS
    per_block = block // tile_lon

    def fetch_op(i):
        return pltpu.make_async_copy(op_hbm.at[:, pl.ds(i * block, block)], op_ref.at[i], op_sem.at[i])

    def fetch_v(f):
        return pltpu.make_async_copy(v_hbm.at[f], v_ref.at[f], v_sem.at[f])

    def store(i):
        part = pl.ds(i * per_block, per_block)
        return pltpu.make_async_copy(out_ref.at[:, part], out_hbm.at[:, part], out_sem.at[i])

    for f in range(fields):
        fetch_v(f).start()
    for i in range(blocks):
        fetch_op(i).start()
    near[...] = stencil(near.shape[0])

    def across(f, carry):
        fetch_v(f).wait()
        side[f] = KAPPA * dot(v_ref[f], near[...])
        return carry

    lax.fori_loop(0, fields, across, 0)
    def step(i, carry):
        fetch_op(i).wait()

        rows_here = pl.ds(pl.multiple_of(i * block, block), block)
        done = []
        for f in range(fields):
            along = dot(op_ref[i], v_ref[f], (0, 0))
            done.append(along + side[f, rows_here, :])
        for a in range(tiles):
            parts = [
                d[:, a * LANES : (a + 1) * LANES].reshape(per_block, chunks, 1, QROWS, LANES)
                for d in done
            ]
            joined = jnp.concatenate(parts, axis=2).reshape(per_block, chunks, rows, LANES)
            out_ref[a, pl.ds(i * per_block, per_block)] = joined.astype(BF)
        store(i).start()
        return carry

    lax.fori_loop(0, blocks, step, 0)
    for i in range(blocks):
        store(i).wait()


def forward(fields_in, operator, lat_tiles, lon_tiles, tile_lon):
    fields, grid_lon, grid_lat = fields_in.shape
    chunks = tile_lon // QROWS
    block = 512
    blocks = grid_lon // block
    out_shape = (lat_tiles, lon_tiles, chunks, fields * QROWS, LANES)
    return pl.pallas_call(
        forward_kernel,
        in_specs=[pl.BlockSpec(memory_space=pltpu.HBM)] * 2,
        out_specs=pl.BlockSpec(memory_space=pltpu.HBM),
        out_shape=pltpu.HBM(out_shape, BF),
        scratch_shapes=[
            pltpu.VMEM(fields_in.shape, BF),
            pltpu.VMEM((blocks, grid_lon, block), BF),
            pltpu.VMEM(out_shape, BF),
            pltpu.VMEM((grid_lat, grid_lat), BF),
            pltpu.VMEM(fields_in.shape, F32),
            pltpu.SemaphoreType.DMA((fields,)),
            pltpu.SemaphoreType.DMA((blocks,)),
            pltpu.SemaphoreType.DMA((blocks,)),
        ],
        compiler_params=params(),
        cost_estimate=cost(2 * fields * grid_lon * grid_lon * grid_lat, 6 << 20),
        name="forward_dynamics",
    )(in_hbm(fields_in), in_hbm(operator))


def grad_mixed_kernel(inv_ref, cot_ref, out_ref, wide):
    levels = inv_ref.shape[0]
    fields = cot_ref.shape[0] // levels
    wide[...] = cot_ref[...].astype(F32)

    def tile(t, carry):
        lanes = pl.ds(pl.multiple_of(t * LANES, LANES), LANES)
        acc = [None] * fields
        for l in range(levels):
            matrix = inv_ref[l, :, lanes].astype(F32)
            for f in range(fields):
                term = matrix * wide[pl.ds(f * levels + l, 1), lanes]
                acc[f] = term if acc[f] is None else acc[f] + term
        for f in range(fields):
            out_ref[f * levels : (f + 1) * levels, lanes] = acc[f].astype(BF)
        return carry

    lax.fori_loop(0, inv_ref.shape[2] // LANES, tile, 0)


def grad_mixed_of(matrix, incoming):
    levels, _, columns = matrix.shape
    values = incoming.shape[0]
    chunk = 512
    return pl.pallas_call(
        grad_mixed_kernel,
        grid=(columns // chunk,),
        in_specs=[
            pl.BlockSpec((levels, levels, chunk), lambda i: (0, 0, i)),
            pl.BlockSpec((values, chunk), lambda i: (0, i)),
        ],
        out_specs=pl.BlockSpec((values, chunk), lambda i: (0, i)),
        out_shape=pltpu.HBM((values, columns), BF),
        scratch_shapes=[pltpu.VMEM((values, chunk), F32)],
        compiler_params=params(40),
        cost_estimate=cost(2 * values * levels * columns, 16 << 20),
        name="grad_mixed",
    )(in_hbm(matrix), in_hbm(incoming))


def network_kernel(
    arrived, gm_hbm, w_half, w_out,
    leaving_hbm, cols_hbm,
    gm, leaving, cols, act, grad_pre, wide_in, wide_out, acc_in, acc_out, gm_sem, out_sem, *, tiles,
):
    sources, steps, rows, _ = arrived.shape
    fields = rows // QROWS
    group = sources // tiles
    chunk = QROWS * LANES
    pitch = wide_in.shape[0] // (sources + 1)

    def fetch(i):
        return pltpu.make_async_copy(gm_hbm.at[:, pl.ds(i * chunk, chunk)], gm.at[i], gm_sem.at[i])

    def store_leaving(i):
        return pltpu.make_async_copy(leaving.at[i], leaving_hbm.at[:, i], out_sem.at[0, i])

    def store_cols(i):
        return pltpu.make_async_copy(
            cols.at[i], cols_hbm.at[:, pl.ds(i * chunk, chunk)], out_sem.at[1, i]
        )

    for i in range(steps):
        fetch(i).start()
    acc_in[...] = jnp.zeros_like(acc_in)
    acc_out[...] = jnp.zeros_like(acc_out)

    def step(i, carry):
        for s in range(sources):
            wide_in[s * pitch : s * pitch + rows, :] = arrived[s, i].astype(F32)
        for q in range(QROWS):
            by_field = [
                wide_in[pl.ds(f * QROWS + q, sources, stride=pitch), :] for f in range(fields)
            ]
            parts = [
                by_field[f][a * group : (a + 1) * group] for a in range(tiles) for f in range(fields)
            ]
            cols[i, :, q * LANES : (q + 1) * LANES] = jnp.concatenate(parts, axis=0).astype(BF)
        half = dot(w_half[...], cols[i])
        turn = jnp.tanh(half)
        value = half + half * turn
        act[...] = value.astype(BF)
        fetch(i).wait()
        slope = 1.0 + (turn + value) - turn * value
        grad_pre[...] = (dot(w_out[...], gm[i], (0, 0)) * slope).astype(BF)
        acc_in[...] += dot(grad_pre[...], cols[i], (1, 1))
        acc_out[...] += dot(act[...], gm[i], (1, 1))
        grad_cols = gm[i].astype(F32) + dot(w_half[...], grad_pre[...], (0, 0))
        for q in range(QROWS):
            piece = grad_cols[:, q * LANES : (q + 1) * LANES]
            for f in range(fields):
                parts = [
                    piece[(a * fields + f) * group : (a * fields + f + 1) * group]
                    for a in range(tiles)
                ]
                wide_out[pl.ds(f * QROWS + q, sources, stride=pitch), :] = jnp.concatenate(
                    parts, axis=0
                )
        for s in range(sources):
            leaving[i, s] = wide_out[s * pitch : s * pitch + rows, :].astype(BF)
        store_cols(i).start()
        store_leaving(i).start()
        return carry

    lax.fori_loop(0, steps, step, 0)
    total_in = 0.5 * acc_in[...]
    total_out = acc_out[...]
    place = 0
    for total in (total_in, total_out):
        height, breadth = total.shape
        for j in range(breadth // LANES):
            count = height // rows
            part = total[:, j * LANES : (j + 1) * LANES].reshape(count, rows, LANES)
            leaving[steps, place : place + count] = part.astype(BF)
            place += count
    store_leaving(steps).start()
    for i in range(steps):
        store_cols(i).wait()
        store_leaving(i).wait()
    store_leaving(steps).wait()


def network(arrived, grad_mixed, w_half, w_out, tiles):
    sources, steps, rows, _ = arrived.shape
    values, columns = grad_mixed.shape
    neurons = w_half.shape[0]
    chunk = columns // steps
    return pl.pallas_call(
        functools.partial(network_kernel, tiles=tiles),
        in_specs=[
            pl.BlockSpec(memory_space=pltpu.VMEM),
            pl.BlockSpec(memory_space=pltpu.HBM),
            pl.BlockSpec(memory_space=pltpu.VMEM),
            pl.BlockSpec(memory_space=pltpu.VMEM),
        ],
        out_specs=[pl.BlockSpec(memory_space=pltpu.HBM)] * 2,
        out_shape=[
            pltpu.HBM((sources, steps + 1, rows, LANES), BF),
            pltpu.HBM((values, columns), BF),
        ],
        scratch_shapes=[
            pltpu.VMEM((steps, values, chunk), BF),
            pltpu.VMEM((steps + 1, sources, rows, LANES), BF),
            pltpu.VMEM((steps, values, chunk), BF),
            pltpu.VMEM((neurons, chunk), BF),
            pltpu.VMEM((neurons, chunk), BF),
            pltpu.VMEM(((sources + 1) * (rows + PAD), LANES), F32),
            pltpu.VMEM(((sources + 1) * (rows + PAD), LANES), F32),
            pltpu.VMEM((neurons, values), F32),
            pltpu.VMEM((neurons, values), F32),
            pltpu.SemaphoreType.DMA((steps,)),
            pltpu.SemaphoreType.DMA((2, steps + 1)),
        ],
        compiler_params=params(40),
        cost_estimate=cost(8 * neurons * values * columns, 14 << 20, neurons * columns),
        name="column_network",
    )(in_vmem(arrived), in_hbm(grad_mixed), in_vmem(w_half), in_vmem(w_out))


def diffused_kernel(cols_ref, w_half_ref, w_out_ref, inv_ref, out_ref, mixed, flat):
    fields, levels = out_ref.shape[0], out_ref.shape[1]
    half = dot(w_half_ref[...], cols_ref[...])
    act = (half + half * jnp.tanh(half)).astype(BF)
    total = cols_ref[...].astype(F32) + dot(w_out_ref[...], act)
    mixed[...] = total.astype(BF).astype(F32)

    def tile(t, carry):
        lanes = pl.ds(pl.multiple_of(t * LANES, LANES), LANES)
        flat[: levels * levels] = inv_ref[:, :, lanes].astype(F32).reshape(levels * levels, LANES)
        acc = [None] * fields
        for m in range(levels):
            matrix = flat[pl.ds(m, levels, stride=levels), :]
            for f in range(fields):
                term = matrix * mixed[pl.ds(f * levels + m, 1), lanes]
                acc[f] = term if acc[f] is None else acc[f] + term
        for f in range(fields):
            out_ref[f, :, lanes] = acc[f]
        return carry

    lax.fori_loop(0, inv_ref.shape[2] // LANES, tile, 0)


def diffused_of(cols, w_half, w_out, matrix, fields):
    levels, _, columns = matrix.shape
    values, neurons = w_out.shape
    chunk = 512
    return pl.pallas_call(
        diffused_kernel,
        grid=(columns // chunk,),
        in_specs=[
            pl.BlockSpec((values, chunk), lambda i: (0, i)),
            pl.BlockSpec((neurons, values), lambda i: (0, 0)),
            pl.BlockSpec((values, neurons), lambda i: (0, 0)),
            pl.BlockSpec((levels, levels, chunk), lambda i: (0, 0, i)),
        ],
        out_specs=pl.BlockSpec((fields, levels, chunk), lambda i: (0, 0, i)),
        out_shape=jax.ShapeDtypeStruct((fields, levels, columns), F32),
        scratch_shapes=[
            pltpu.VMEM((values, chunk), F32),
            pltpu.VMEM(((levels + 1) * levels, LANES), F32),
        ],
        compiler_params=params(),
        cost_estimate=cost(2 * values * (levels + 2 * neurons) * columns, 16 << 20),
        name="diffused",
    )(in_hbm(cols), w_half, w_out, in_hbm(matrix))


def adjoint_kernel(back, op_hbm, out_hbm, op_ref, grid_ref, out_ref, op_sem, out_sem):
    fields = out_ref.shape[0]
    tiles, lon_tiles = back.shape[:2]
    grid_lon = grid_ref.shape[1]
    chunks = grid_lon // (lon_tiles * QROWS)
    block = 256
    blocks = grid_lon // block

    def fetch_op(i):
        part = pl.ds(i * block, block)
        return pltpu.make_async_copy(op_hbm.at[part], op_ref.at[part], op_sem.at[i])

    def store(f, i):
        part = pl.ds(i * block, block)
        return pltpu.make_async_copy(out_ref.at[f, part], out_hbm.at[f, part], out_sem.at[f, i])

    for i in range(blocks):
        fetch_op(i).start()
    for a in range(tiles):
        wide = back[a, :, :chunks].astype(F32).reshape(lon_tiles * chunks, fields, QROWS, LANES)
        for f in range(fields):
            grid_ref[f, :, a * LANES : (a + 1) * LANES] = (
                wide[:, f].reshape(grid_lon, LANES).astype(BF)
            )
    def step(i, carry):
        fetch_op(i).wait()
        part = pl.ds(pl.multiple_of(i * block, block), block)
        for f in range(fields):
            along = dot(op_ref[part, :], grid_ref[f])
            wide = grid_ref[f, part, :].astype(F32)
            out_ref[f, part, :] = along + spread(wide)
            store(f, i).start()
        return carry

    lax.fori_loop(0, blocks, step, 0)
    for i in range(blocks):
        for f in range(fields):
            store(f, i).wait()


def adjoint(returned, operator, fields, grid_lat):
    grid_lon = operator.shape[0]
    blocks = grid_lon // 256
    return pl.pallas_call(
        adjoint_kernel,
        in_specs=[pl.BlockSpec(memory_space=pltpu.VMEM), pl.BlockSpec(memory_space=pltpu.HBM)],
        out_specs=pl.BlockSpec(memory_space=pltpu.HBM),
        out_shape=jax.ShapeDtypeStruct((fields, grid_lon, grid_lat), F32),
        scratch_shapes=[
            pltpu.VMEM(operator.shape, BF),
            pltpu.VMEM((fields, grid_lon, grid_lat), BF),
            pltpu.VMEM((fields, grid_lon, grid_lat), F32),
            pltpu.SemaphoreType.DMA((blocks,)),
            pltpu.SemaphoreType.DMA((fields, blocks)),
        ],
        compiler_params=params(48),
        cost_estimate=cost(2 * fields * grid_lon * grid_lon * grid_lat, 8 << 20),
        name="adjoint_dynamics",
    )(in_vmem(returned), in_hbm(operator))


def weight_sum_kernel(returned, _, out_hbm, out_ref, out_sem):
    last = returned.shape[1] - 1
    sources = out_ref.shape[0]
    lanes = 8
    partial = [returned[k, last].astype(F32) for k in range(lanes)]
    for k in range(lanes, sources):
        partial[k % lanes] = partial[k % lanes] + returned[k, last].astype(F32)
    while len(partial) > 1:
        partial = [a + b for a, b in zip(partial[::2], partial[1::2])]
    total = partial[0].astype(BF)
    pieces = out_sem.shape[0]
    each = sources // pieces

    def store(k):
        part = pl.ds(k * each, each)
        return pltpu.make_async_copy(out_ref.at[part], out_hbm.at[part], out_sem.at[k])

    for k in range(pieces):
        out_ref[k * each : (k + 1) * each] = jnp.broadcast_to(total[None], (each,) + total.shape)
        store(k).start()
    for k in range(pieces):
        store(k).wait()


def weight_sum(returned, after):
    sources, _, rows, _ = returned.shape
    shape = (sources, rows, LANES)
    return pl.pallas_call(
        weight_sum_kernel,
        in_specs=[pl.BlockSpec(memory_space=pltpu.VMEM), pl.BlockSpec(memory_space=pltpu.HBM)],
        out_specs=pl.BlockSpec(memory_space=pltpu.HBM),
        out_shape=pltpu.HBM(shape, BF),
        scratch_shapes=[pltpu.VMEM(shape, BF), pltpu.SemaphoreType.DMA((1,))],
        compiler_params=params(48),
        cost_estimate=cost(sources * rows * LANES, 1 << 20),
        name="weight_sum",
    )(in_vmem(returned), in_hbm(after))


def weight_spread_kernel(shares, in_hbm, out_hbm, in_ref, out_ref, out_sem):
    rows = shares.shape[1]
    height, breadth = in_ref.shape
    count = height // rows
    each = breadth // LANES
    jobs = 2 * each

    def store(k):
        part = pl.ds((k % each) * LANES, LANES)
        if k < each:
            return pltpu.make_async_copy(in_ref.at[:, part], in_hbm.at[:, part], out_sem.at[k])
        return pltpu.make_async_copy(out_ref.at[part], out_hbm.at[part], out_sem.at[k])

    for k in range(jobs):
        wide = shares[k * count : (k + 1) * count].astype(F32).reshape(height, LANES)
        part = slice((k % each) * LANES, (k % each + 1) * LANES)
        if k < each:
            in_ref[:, part] = wide
        else:
            out_ref[part, :] = wide.T
        store(k).start()
    for k in range(jobs):
        store(k).wait()


def weight_spread(shares, neurons, values):
    shapes = [(neurons, values), (values, neurons)]
    jobs = 2 * (values // LANES)
    return pl.pallas_call(
        weight_spread_kernel,
        in_specs=[pl.BlockSpec(memory_space=pltpu.VMEM)],
        out_specs=[pl.BlockSpec(memory_space=pltpu.HBM)] * 2,
        out_shape=[jax.ShapeDtypeStruct(shape, F32) for shape in shapes],
        scratch_shapes=[pltpu.VMEM(shape, F32) for shape in shapes]
        + [pltpu.SemaphoreType.DMA((jobs,))],
        compiler_params=params(48),
        name="weight_spread",
    )(in_vmem(shares))


def exchange(array):
    return lax.all_to_all(array, AXES, split_axis=0, concat_axis=0, tiled=True)


def per_device(fields_in, lon_operator, w_in, w_out, inverses, cotangent):
    lat_tiles = lax.axis_size("lat")
    lon_tiles = lax.axis_size("lon")
    devices = lat_tiles * lon_tiles
    field_dev, _, grid_lon, grid_lat = fields_in.shape
    all_fields, all_levels, columns = cotangent.shape[2:]
    neurons, values = w_in.shape
    tile_lon = grid_lon // lon_tiles

    leaving = forward(
        fields_in.reshape(field_dev, grid_lon, grid_lat), lon_operator, lat_tiles, lon_tiles, tile_lon
    )
    arrived = exchange(leaving.reshape((devices,) + leaving.shape[2:]))

    matrix = inverses.reshape(all_levels, all_levels, columns)
    w_half = 0.5 * w_in
    grad_mixed = grad_mixed_of(matrix, cotangent.reshape(values, columns))

    going, cols = network(arrived, grad_mixed, w_half, w_out, lat_tiles)
    returned = exchange(going)

    diffused = diffused_of(cols, w_half, w_out, matrix, all_fields)

    shares = exchange(weight_sum(returned, diffused))
    grad_fields = adjoint(
        returned.reshape((lat_tiles, lon_tiles) + returned.shape[1:]), lon_operator, field_dev, grid_lat
    )
    grad_in, grad_out = weight_spread(shares, neurons, values)
    return (
        diffused.reshape(1, 1, all_fields, all_levels, columns),
        grad_fields.reshape(field_dev, 1, grid_lon, grid_lat),
        grad_in,
        grad_out,
    )


def solution(mesh):
    in_specs = (
        P("lat", "lon", None, None),
        P(),
        P(),
        P(),
        P("lat", "lon", None, None, None),
        P("lat", "lon", None, None, None),
    )
    out_specs = (P("lat", "lon", None, None, None), P("lat", "lon", None, None), P(), P())
    return jax.shard_map(
        per_device, mesh=mesh, in_specs=in_specs, out_specs=out_specs, check_vma=False
    )
```

```python
import functools

import jax
import jax.numpy as jnp
from jax import lax
from jax.experimental import pallas as pl
from jax.experimental.pallas import tpu as pltpu
from jax.sharding import PartitionSpec as P

KAPPA = 0.2
AXES = ("lat", "lon")
BF = jnp.bfloat16
F32 = jnp.float32
LANES = 128
QROWS = 8
PAD = 8


def params(mebibytes=60):
    return pltpu.CompilerParams(vmem_limit_bytes=mebibytes * 1024 * 1024)


def in_vmem(x):
    return pltpu.with_memory_space_constraint(x, pltpu.VMEM)


def in_hbm(x):
    return pltpu.with_memory_space_constraint(x, pltpu.HBM)


def cost(flops, nbytes, trans=0):
    return pl.CostEstimate(flops=int(flops), bytes_accessed=int(nbytes), transcendentals=int(trans))


def dot(a, b, dims=(1, 0)):
    return lax.dot_general(a, b, (((dims[0],), (dims[1],)), ((), ())), preferred_element_type=F32)


def stencil(size):
    row = lax.broadcasted_iota(jnp.int32, (size, size), 0)
    lane = lax.broadcasted_iota(jnp.int32, (size, size), 1)
    apart = jnp.abs(row - lane)
    return jnp.where(apart == 0, 1.0 / KAPPA - 2.0, jnp.where(apart == 1, 1.0, 0.0)).astype(BF)


def spread(wide):
    size = wide.shape[1]
    lane = lax.broadcasted_iota(jnp.int32, wide.shape, 1)
    before = jnp.where(lane == 0, 0.0, pltpu.roll(wide, 1, 1))
    after = jnp.where(lane == size - 1, 0.0, pltpu.roll(wide, size - 1, 1))
    return (1.0 - 2.0 * KAPPA) * wide + KAPPA * (after + before)


def forward_kernel(v_hbm, op_hbm, out_hbm, v_ref, op_ref, out_ref, near, side, v_sem, op_sem, out_sem):
    fields = v_ref.shape[0]
    blocks = op_ref.shape[0]
    block = op_ref.shape[2]
    tiles, _, chunks, rows, _ = out_ref.shape
    tile_lon = chunks * QROWS
    per_block = block // tile_lon

    def fetch_op(i):
        return pltpu.make_async_copy(op_hbm.at[:, pl.ds(i * block, block)], op_ref.at[i], op_sem.at[i])

    def fetch_v(f):
        return pltpu.make_async_copy(v_hbm.at[f], v_ref.at[f], v_sem.at[f])

    half = tiles // 2
    width = half * LANES

    def store(k):
        across, part = pl.ds((k % 2) * half, half), pl.ds((k // 2) * per_block, per_block)
        return pltpu.make_async_copy(
            out_ref.at[across, part], out_hbm.at[across, part], out_sem.at[k]
        )

    for f in range(fields):
        fetch_v(f).start()
    for i in range(blocks):
        fetch_op(i).start()
    near[...] = stencil(near.shape[0])

    def across(f, carry):
        fetch_v(f).wait()
        side[f] = KAPPA * dot(v_ref[f], near[...])
        return carry

    lax.fori_loop(0, fields, across, 0)
    def step(k, carry):
        i, h = k // 2, k % 2

        @pl.when(h == 0)
        def _():
            fetch_op(i).wait()

        rows_here = pl.ds(pl.multiple_of(i * block, block), block)
        lanes = pl.ds(pl.multiple_of(h * width, width), width)
        done = []
        for f in range(fields):
            along = dot(op_ref[i], v_ref[f, :, lanes], (0, 0))
            done.append(along + side[f, rows_here, lanes])
        for a in range(half):
            parts = [
                d[:, a * LANES : (a + 1) * LANES].reshape(per_block, chunks, 1, QROWS, LANES)
                for d in done
            ]
            joined = jnp.concatenate(parts, axis=2).reshape(per_block, chunks, rows, LANES)
            out_ref[h * half + a, pl.ds(i * per_block, per_block)] = joined.astype(BF)
        store(k).start()
        return carry

    lax.fori_loop(0, 2 * blocks, step, 0)
    for k in range(2 * blocks):
        store(k).wait()


def forward(fields_in, operator, lat_tiles, lon_tiles, tile_lon):
    fields, grid_lon, grid_lat = fields_in.shape
    chunks = tile_lon // QROWS
    block = 512
    blocks = grid_lon // block
    out_shape = (lat_tiles, lon_tiles, chunks, fields * QROWS, LANES)
    return pl.pallas_call(
        forward_kernel,
        in_specs=[pl.BlockSpec(memory_space=pltpu.HBM)] * 2,
        out_specs=pl.BlockSpec(memory_space=pltpu.HBM),
        out_shape=pltpu.HBM(out_shape, BF),
        scratch_shapes=[
            pltpu.VMEM(fields_in.shape, BF),
            pltpu.VMEM((blocks, grid_lon, block), BF),
            pltpu.VMEM(out_shape, BF),
            pltpu.VMEM((grid_lat, grid_lat), BF),
            pltpu.VMEM(fields_in.shape, F32),
            pltpu.SemaphoreType.DMA((fields,)),
            pltpu.SemaphoreType.DMA((blocks,)),
            pltpu.SemaphoreType.DMA((2 * blocks,)),
        ],
        compiler_params=params(),
        cost_estimate=cost(2 * fields * grid_lon * grid_lon * grid_lat, 6 << 20),
        name="forward_dynamics",
    )(in_hbm(fields_in), in_hbm(operator))


def grad_mixed_kernel(inv_ref, cot_ref, out_ref, wide):
    levels = inv_ref.shape[0]
    fields = cot_ref.shape[0] // levels
    wide[...] = cot_ref[...].astype(F32)

    def tile(t, carry):
        lanes = pl.ds(pl.multiple_of(t * LANES, LANES), LANES)
        acc = [None] * fields
        for l in range(levels):
            matrix = inv_ref[l, :, lanes].astype(F32)
            for f in range(fields):
                term = matrix * wide[pl.ds(f * levels + l, 1), lanes]
                acc[f] = term if acc[f] is None else acc[f] + term
        for f in range(fields):
            out_ref[f * levels : (f + 1) * levels, lanes] = acc[f].astype(BF)
        return carry

    lax.fori_loop(0, inv_ref.shape[2] // LANES, tile, 0)


def grad_mixed_of(matrix, incoming):
    levels, _, columns = matrix.shape
    values = incoming.shape[0]
    chunk = 512
    return pl.pallas_call(
        grad_mixed_kernel,
        grid=(columns // chunk,),
        in_specs=[
            pl.BlockSpec((levels, levels, chunk), lambda i: (0, 0, i)),
            pl.BlockSpec((values, chunk), lambda i: (0, i)),
        ],
        out_specs=pl.BlockSpec((values, chunk), lambda i: (0, i)),
        out_shape=pltpu.HBM((values, columns), BF),
        scratch_shapes=[pltpu.VMEM((values, chunk), F32)],
        compiler_params=params(40),
        cost_estimate=cost(2 * values * levels * columns, 16 << 20),
        name="grad_mixed",
    )(in_hbm(matrix), in_hbm(incoming))


def network_kernel(
    arrived, gm_hbm, w_half, w_out,
    leaving_hbm, cols_hbm,
    gm, leaving, cols, act, grad_pre, wide_in, wide_out, acc_in, acc_out, gm_sem, out_sem, *, tiles,
):
    sources, steps, rows, _ = arrived.shape
    fields = rows // QROWS
    group = sources // tiles
    chunk = QROWS * LANES
    pitch = wide_in.shape[0] // (sources + 1)

    def fetch(i):
        return pltpu.make_async_copy(gm_hbm.at[:, pl.ds(i * chunk, chunk)], gm.at[i], gm_sem.at[i])

    def store_leaving(i):
        return pltpu.make_async_copy(leaving.at[i], leaving_hbm.at[:, i], out_sem.at[0, i])

    def store_cols(i):
        return pltpu.make_async_copy(
            cols.at[i], cols_hbm.at[:, pl.ds(i * chunk, chunk)], out_sem.at[1, i]
        )

    for i in range(steps):
        fetch(i).start()
    acc_in[...] = jnp.zeros_like(acc_in)
    acc_out[...] = jnp.zeros_like(acc_out)

    def step(i, carry):
        for s in range(sources):
            wide_in[s * pitch : s * pitch + rows, :] = arrived[s, i].astype(F32)
        for q in range(QROWS):
            by_field = [
                wide_in[pl.ds(f * QROWS + q, sources, stride=pitch), :] for f in range(fields)
            ]
            parts = [
                by_field[f][a * group : (a + 1) * group] for a in range(tiles) for f in range(fields)
            ]
            cols[i, :, q * LANES : (q + 1) * LANES] = jnp.concatenate(parts, axis=0).astype(BF)
        half = dot(w_half[...], cols[i])
        turn = jnp.tanh(half)
        value = half + half * turn
        act[...] = value.astype(BF)
        fetch(i).wait()
        slope = 1.0 + (turn + value) - turn * value
        grad_pre[...] = (dot(w_out[...], gm[i], (0, 0)) * slope).astype(BF)
        acc_in[...] += dot(grad_pre[...], cols[i], (1, 1))
        acc_out[...] += dot(act[...], gm[i], (1, 1))
        grad_cols = gm[i].astype(F32) + dot(w_half[...], grad_pre[...], (0, 0))
        for q in range(QROWS):
            piece = grad_cols[:, q * LANES : (q + 1) * LANES]
            for f in range(fields):
                parts = [
                    piece[(a * fields + f) * group : (a * fields + f + 1) * group]
                    for a in range(tiles)
                ]
                wide_out[pl.ds(f * QROWS + q, sources, stride=pitch), :] = jnp.concatenate(
                    parts, axis=0
                )
        for s in range(sources):
            leaving[i, s] = wide_out[s * pitch : s * pitch + rows, :].astype(BF)
        store_cols(i).start()
        store_leaving(i).start()
        return carry

    lax.fori_loop(0, steps, step, 0)
    total_in = 0.5 * acc_in[...]
    total_out = acc_out[...]
    place = 0
    for total in (total_in, total_out):
        height, breadth = total.shape
        for j in range(breadth // LANES):
            count = height // rows
            part = total[:, j * LANES : (j + 1) * LANES].reshape(count, rows, LANES)
            leaving[steps, place : place + count] = part.astype(BF)
            place += count
    store_leaving(steps).start()
    for i in range(steps):
        store_cols(i).wait()
        store_leaving(i).wait()
    store_leaving(steps).wait()


def network(arrived, grad_mixed, w_half, w_out, tiles):
    sources, steps, rows, _ = arrived.shape
    values, columns = grad_mixed.shape
    neurons = w_half.shape[0]
    chunk = columns // steps
    return pl.pallas_call(
        functools.partial(network_kernel, tiles=tiles),
        in_specs=[
            pl.BlockSpec(memory_space=pltpu.VMEM),
            pl.BlockSpec(memory_space=pltpu.HBM),
            pl.BlockSpec(memory_space=pltpu.VMEM),
            pl.BlockSpec(memory_space=pltpu.VMEM),
        ],
        out_specs=[pl.BlockSpec(memory_space=pltpu.HBM)] * 2,
        out_shape=[
            pltpu.HBM((sources, steps + 1, rows, LANES), BF),
            pltpu.HBM((values, columns), BF),
        ],
        scratch_shapes=[
            pltpu.VMEM((steps, values, chunk), BF),
            pltpu.VMEM((steps + 1, sources, rows, LANES), BF),
            pltpu.VMEM((steps, values, chunk), BF),
            pltpu.VMEM((neurons, chunk), BF),
            pltpu.VMEM((neurons, chunk), BF),
            pltpu.VMEM(((sources + 1) * (rows + PAD), LANES), F32),
            pltpu.VMEM(((sources + 1) * (rows + PAD), LANES), F32),
            pltpu.VMEM((neurons, values), F32),
            pltpu.VMEM((neurons, values), F32),
            pltpu.SemaphoreType.DMA((steps,)),
            pltpu.SemaphoreType.DMA((2, steps + 1)),
        ],
        compiler_params=params(40),
        cost_estimate=cost(8 * neurons * values * columns, 14 << 20, neurons * columns),
        name="column_network",
    )(in_vmem(arrived), in_hbm(grad_mixed), in_vmem(w_half), in_vmem(w_out))


def diffused_kernel(cols_ref, w_half_ref, w_out_ref, inv_ref, out_ref, mixed, flat):
    fields, levels = out_ref.shape[0], out_ref.shape[1]
    half = dot(w_half_ref[...], cols_ref[...])
    act = (half + half * jnp.tanh(half)).astype(BF)
    total = cols_ref[...].astype(F32) + dot(w_out_ref[...], act)
    mixed[...] = total.astype(BF).astype(F32)

    def tile(t, carry):
        lanes = pl.ds(pl.multiple_of(t * LANES, LANES), LANES)
        flat[: levels * levels] = inv_ref[:, :, lanes].astype(F32).reshape(levels * levels, LANES)
        acc = [None] * fields
        for m in range(levels):
            matrix = flat[pl.ds(m, levels, stride=levels), :]
            for f in range(fields):
                term = matrix * mixed[pl.ds(f * levels + m, 1), lanes]
                acc[f] = term if acc[f] is None else acc[f] + term
        for f in range(fields):
            out_ref[f, :, lanes] = acc[f]
        return carry

    lax.fori_loop(0, inv_ref.shape[2] // LANES, tile, 0)


def diffused_of(cols, w_half, w_out, matrix, fields):
    levels, _, columns = matrix.shape
    values, neurons = w_out.shape
    chunk = 512
    return pl.pallas_call(
        diffused_kernel,
        grid=(columns // chunk,),
        in_specs=[
            pl.BlockSpec((values, chunk), lambda i: (0, i)),
            pl.BlockSpec((neurons, values), lambda i: (0, 0)),
            pl.BlockSpec((values, neurons), lambda i: (0, 0)),
            pl.BlockSpec((levels, levels, chunk), lambda i: (0, 0, i)),
        ],
        out_specs=pl.BlockSpec((fields, levels, chunk), lambda i: (0, 0, i)),
        out_shape=jax.ShapeDtypeStruct((fields, levels, columns), F32),
        scratch_shapes=[
            pltpu.VMEM((values, chunk), F32),
            pltpu.VMEM(((levels + 1) * levels, LANES), F32),
        ],
        compiler_params=params(),
        cost_estimate=cost(2 * values * (levels + 2 * neurons) * columns, 16 << 20),
        name="diffused",
    )(in_hbm(cols), w_half, w_out, in_hbm(matrix))


def adjoint_kernel(back, op_hbm, out_hbm, op_ref, grid_ref, out_ref, op_sem, out_sem):
    fields = out_ref.shape[0]
    tiles, lon_tiles = back.shape[:2]
    grid_lon = grid_ref.shape[1]
    chunks = grid_lon // (lon_tiles * QROWS)
    block = 256
    blocks = grid_lon // block

    def fetch_op(i):
        part = pl.ds(i * block, block)
        return pltpu.make_async_copy(op_hbm.at[part], op_ref.at[part], op_sem.at[i])

    def store(f, i):
        part = pl.ds(i * block, block)
        return pltpu.make_async_copy(out_ref.at[f, part], out_hbm.at[f, part], out_sem.at[f, i])

    for i in range(blocks):
        fetch_op(i).start()
    for a in range(tiles):
        wide = back[a, :, :chunks].astype(F32).reshape(lon_tiles * chunks, fields, QROWS, LANES)
        for f in range(fields):
            grid_ref[f, :, a * LANES : (a + 1) * LANES] = (
                wide[:, f].reshape(grid_lon, LANES).astype(BF)
            )
    def step(i, carry):
        fetch_op(i).wait()
        part = pl.ds(pl.multiple_of(i * block, block), block)
        for f in range(fields):
            along = dot(op_ref[part, :], grid_ref[f])
            wide = grid_ref[f, part, :].astype(F32)
            out_ref[f, part, :] = along + spread(wide)
            store(f, i).start()
        return carry

    lax.fori_loop(0, blocks, step, 0)
    for i in range(blocks):
        for f in range(fields):
            store(f, i).wait()


def adjoint(returned, operator, fields, grid_lat):
    grid_lon = operator.shape[0]
    blocks = grid_lon // 256
    return pl.pallas_call(
        adjoint_kernel,
        in_specs=[pl.BlockSpec(memory_space=pltpu.VMEM), pl.BlockSpec(memory_space=pltpu.HBM)],
        out_specs=pl.BlockSpec(memory_space=pltpu.HBM),
        out_shape=jax.ShapeDtypeStruct((fields, grid_lon, grid_lat), F32),
        scratch_shapes=[
            pltpu.VMEM(operator.shape, BF),
            pltpu.VMEM((fields, grid_lon, grid_lat), BF),
            pltpu.VMEM((fields, grid_lon, grid_lat), F32),
            pltpu.SemaphoreType.DMA((blocks,)),
            pltpu.SemaphoreType.DMA((fields, blocks)),
        ],
        compiler_params=params(48),
        cost_estimate=cost(2 * fields * grid_lon * grid_lon * grid_lat, 8 << 20),
        name="adjoint_dynamics",
    )(in_vmem(returned), in_hbm(operator))


def weight_sum_kernel(returned, _, out_hbm, out_ref, out_sem):
    last = returned.shape[1] - 1
    sources = out_ref.shape[0]
    lanes = 8
    partial = [returned[k, last].astype(F32) for k in range(lanes)]
    for k in range(lanes, sources):
        partial[k % lanes] = partial[k % lanes] + returned[k, last].astype(F32)
    while len(partial) > 1:
        partial = [a + b for a, b in zip(partial[::2], partial[1::2])]
    total = partial[0].astype(BF)
    pieces = out_sem.shape[0]
    each = sources // pieces

    def store(k):
        part = pl.ds(k * each, each)
        return pltpu.make_async_copy(out_ref.at[part], out_hbm.at[part], out_sem.at[k])

    for k in range(pieces):
        out_ref[k * each : (k + 1) * each] = jnp.broadcast_to(total[None], (each,) + total.shape)
        store(k).start()
    for k in range(pieces):
        store(k).wait()


def weight_sum(returned, after):
    sources, _, rows, _ = returned.shape
    shape = (sources, rows, LANES)
    return pl.pallas_call(
        weight_sum_kernel,
        in_specs=[pl.BlockSpec(memory_space=pltpu.VMEM), pl.BlockSpec(memory_space=pltpu.HBM)],
        out_specs=pl.BlockSpec(memory_space=pltpu.HBM),
        out_shape=pltpu.HBM(shape, BF),
        scratch_shapes=[pltpu.VMEM(shape, BF), pltpu.SemaphoreType.DMA((1,))],
        compiler_params=params(48),
        cost_estimate=cost(sources * rows * LANES, 1 << 20),
        name="weight_sum",
    )(in_vmem(returned), in_hbm(after))


def weight_spread_kernel(shares, in_hbm, out_hbm, in_ref, out_ref, out_sem):
    rows = shares.shape[1]
    height, breadth = in_ref.shape
    count = height // rows
    each = breadth // LANES
    jobs = 2 * each

    def store(k):
        part = pl.ds((k % each) * LANES, LANES)
        if k < each:
            return pltpu.make_async_copy(in_ref.at[:, part], in_hbm.at[:, part], out_sem.at[k])
        return pltpu.make_async_copy(out_ref.at[part], out_hbm.at[part], out_sem.at[k])

    for k in range(jobs):
        wide = shares[k * count : (k + 1) * count].astype(F32).reshape(height, LANES)
        part = slice((k % each) * LANES, (k % each + 1) * LANES)
        if k < each:
            in_ref[:, part] = wide
        else:
            out_ref[part, :] = wide.T
        store(k).start()
    for k in range(jobs):
        store(k).wait()


def weight_spread(shares, neurons, values):
    shapes = [(neurons, values), (values, neurons)]
    jobs = 2 * (values // LANES)
    return pl.pallas_call(
        weight_spread_kernel,
        in_specs=[pl.BlockSpec(memory_space=pltpu.VMEM)],
        out_specs=[pl.BlockSpec(memory_space=pltpu.HBM)] * 2,
        out_shape=[jax.ShapeDtypeStruct(shape, F32) for shape in shapes],
        scratch_shapes=[pltpu.VMEM(shape, F32) for shape in shapes]
        + [pltpu.SemaphoreType.DMA((jobs,))],
        compiler_params=params(48),
        name="weight_spread",
    )(in_vmem(shares))


def exchange(array):
    return lax.all_to_all(array, AXES, split_axis=0, concat_axis=0, tiled=True)


def per_device(fields_in, lon_operator, w_in, w_out, inverses, cotangent):
    lat_tiles = lax.axis_size("lat")
    lon_tiles = lax.axis_size("lon")
    devices = lat_tiles * lon_tiles
    field_dev, _, grid_lon, grid_lat = fields_in.shape
    all_fields, all_levels, columns = cotangent.shape[2:]
    neurons, values = w_in.shape
    tile_lon = grid_lon // lon_tiles

    leaving = forward(
        fields_in.reshape(field_dev, grid_lon, grid_lat), lon_operator, lat_tiles, lon_tiles, tile_lon
    )
    arrived = exchange(leaving.reshape((devices,) + leaving.shape[2:]))

    matrix = inverses.reshape(all_levels, all_levels, columns)
    w_half = 0.5 * w_in
    grad_mixed = grad_mixed_of(matrix, cotangent.reshape(values, columns))

    going, cols = network(arrived, grad_mixed, w_half, w_out, lat_tiles)
    returned = exchange(going)

    diffused = diffused_of(cols, w_half, w_out, matrix, all_fields)

    shares = exchange(weight_sum(returned, diffused))
    grad_fields = adjoint(
        returned.reshape((lat_tiles, lon_tiles) + returned.shape[1:]), lon_operator, field_dev, grid_lat
    )
    grad_in, grad_out = weight_spread(shares, neurons, values)
    return (
        diffused.reshape(1, 1, all_fields, all_levels, columns),
        grad_fields.reshape(field_dev, 1, grid_lon, grid_lat),
        grad_in,
        grad_out,
    )


def solution(mesh):
    in_specs = (
        P("lat", "lon", None, None),
        P(),
        P(),
        P(),
        P("lat", "lon", None, None, None),
        P("lat", "lon", None, None, None),
    )
    out_specs = (P("lat", "lon", None, None, None), P("lat", "lon", None, None), P(), P())
    return jax.shard_map(
        per_device, mesh=mesh, in_specs=in_specs, out_specs=out_specs, check_vma=False
    )
```
